32 devices in a mesh: loop: 16 (over z, y, core), grp: 2 (over x).
Axes of the slice: x: 2, y: 2, z: 4, core: 2. Of those that a mesh axis runs over, the one named last changes fastest.
Arguments:
- ratings: bfloat16 [2, 16384, 2048], P(None, ('loop', 'grp')), may hold values from -2.5 to 2.5, as said below
- user_factors: float32 [16384, 128], P(('loop', 'grp')), may hold values from -2 to 2
- user_accum: float32 [16384, 128], P(('loop', 'grp')), may hold values from 20 to 400
- item_factors: float32 [32768, 128], P('loop'), may hold values from -2 to 2
- item_accum: float32 [32768, 128], P('loop'), may hold values from 20 to 400
Outputs:
- users_out: float32 [16384, 128], P(('loop', 'grp'))
- items_out: float32 [32768, 128], P('loop')
The draws below stay inside these ranges and needn't reach their ends.
Inputs may be any that keep to these rules, and one draw needn't show every extreme that they name: `ratings`: each entry is 0 (unobserved) or has magnitude 0.5 or more.
All inputs are finite; a program needn't handle non-finite values.
Results may differ from the reference program's by a relative error of at most 0.0085.
Values may be sent and summed in bfloat16 or wider, within the bound.
No kernel may reach another device: no remote copies, remote signals or barrier semaphores. Data moves between devices by JAX's collectives and lax.ppermute only.
A program may use at most 64 MiB of HBM per device.

```python
import math
import jax
import jax.numpy as jnp
from jax import lax

K = 128
UD = 512
IB = 2048
SUB = 2
INNER = 2
USERS = 16384
ITEMS = 32768
N_LOOP = 16
N_GRP = 2


def draw_ratings(key, part):
    keys = jax.random.split(jax.random.fold_in(key, 17), 5)
    row_log = jax.random.uniform(keys[0], (1, USERS, 1), minval=math.log(0.05), maxval=math.log(0.6))
    col_log = jax.random.uniform(keys[1], (1, 1, IB), minval=math.log(0.5), maxval=0.0)
    density = jnp.exp(row_log + col_log)
    keep = jax.random.uniform(keys[2], (SUB, USERS, IB)) < density
    magnitude = jax.random.uniform(keys[3], (SUB, USERS, IB), minval=0.5, maxval=2.5)
    positive = jax.random.uniform(keys[4], (SUB, USERS, IB)) < 0.5
    signed = jnp.where(positive, magnitude, -magnitude)
    return jnp.where(keep, signed, 0.0).astype(jnp.bfloat16)


def level_of(key, shape, cuts, low, largest):
    level = 1.0
    for axis_at, parts in cuts:
        heights = jax.random.uniform(jax.random.fold_in(jax.random.fold_in(key, 6), axis_at), (parts,), jnp.float32, low / len(cuts), largest / len(cuts))
        level = level * jnp.repeat(jnp.exp(heights), shape[axis_at] // parts).reshape((-1,) + (1,) * (len(shape) - 1 - axis_at))
    return level


def normal_values(rng, extent, spread, limit, shards=(), kind=jnp.bfloat16):
    values = jax.random.normal(rng, extent, jnp.float32) * spread
    if len(shards) > 0:
        values = level_of(rng, extent, shards, -0.22, 0.18) * values
    return jnp.clip(values, min=-limit, max=limit).astype(kind)


def setup_inputs(seed: int = 0) -> dict:
    streams_of = jax.random.split(jax.random.key(seed), 6)
    return {
        "ratings": draw_ratings(jax.random.fold_in(streams_of[5], 71), 0),
        "user_factors": normal_values(streams_of[1], (USERS, K), 0.3, 2.0, ((0, 32),), jnp.float32),
        "user_accum": jnp.clip(jnp.exp(math.log(400.0) - 2.9957323 * jax.random.uniform(streams_of[2], (USERS, K), jnp.float32) ** level_of(streams_of[2], (USERS, K), ((0, 32),), -0.2, 0.2)), 20.0, 400.0),
        "item_factors": normal_values(streams_of[3], (ITEMS, K), 0.3, 2.0, ((0, 16),), jnp.float32),
        "item_accum": jnp.clip(jnp.exp(math.log(400.0) - 2.9957323 * jax.random.uniform(streams_of[4], (ITEMS, K), jnp.float32) ** level_of(streams_of[4], (ITEMS, K), ((0, 16),), -0.2, 0.2)), 20.0, 400.0),
    }


shrink = 0.05
learn_rate = 0.2
tiny_eps = 1e-06

def worker_pass(operands):
    users, user_acc, items, item_acc, rates = operands
    rate_full = rates.astype(jnp.float32)
    observed = (jnp.abs(rate_full) > 0.25).astype(jnp.float32)
    for inner_step in range(INNER):
        user_half = users.astype(jnp.bfloat16)
        item_half = items.astype(jnp.bfloat16)
        predicted = jnp.dot(user_half, item_half.T, preferred_element_type=jnp.float32)
        resid = (observed * (rate_full - predicted)).astype(jnp.bfloat16)
        grad_user = -jnp.dot(resid, item_half, preferred_element_type=jnp.float32) + shrink * users
        terms = jnp.einsum('gui,guk->gik', resid.reshape(N_GRP, UD, IB).astype(jnp.float32), user_half.reshape(N_GRP, UD, K).astype(jnp.float32))
        rounded = lax.optimization_barrier((-terms).astype(jnp.bfloat16))
        grad_item = lax.optimization_barrier(jnp.sum(rounded.astype(jnp.float32), axis=0)) + shrink * items
        user_acc = user_acc + grad_user * grad_user
        users = users - learn_rate * grad_user / jnp.sqrt(user_acc + tiny_eps)
        item_acc = item_acc + grad_item * grad_item
        items = items - learn_rate * grad_item / jnp.sqrt(item_acc + tiny_eps)
    return (users, user_acc, items, item_acc)

def reference(ratings, user_factors, user_accum, item_factors, item_accum):
    users = user_factors.reshape(N_LOOP, N_GRP * UD, K)
    user_acc = user_accum.reshape(N_LOOP, N_GRP * UD, K)
    items = item_factors.reshape(N_LOOP, IB, K)
    item_acc = item_accum.reshape(N_LOOP, IB, K)
    rates = ratings.reshape(SUB, N_LOOP, N_GRP * UD, IB)
    for sub_epoch in range(SUB):
        if sub_epoch > 0:
            items = jnp.roll(items, 1, axis=0)
            item_acc = jnp.roll(item_acc, 1, axis=0)
        users, user_acc, items, item_acc = lax.map(worker_pass, (users, user_acc, items, item_acc, rates[sub_epoch]))
    return (users.reshape(USERS, K), items.reshape(ITEMS, K))
```

```python
import jax
import jax.numpy as jnp
from jax import lax
from jax.sharding import PartitionSpec as P

SUB = 2
INNER = 2
CHUNKS = 4


shrink = 0.05
learn_rate = 0.2
tiny_eps = 1e-06


def shifted(shard, axis, by):
    devices = lax.axis_size(axis)
    return lax.ppermute(shard, axis, [(i, (i + by) % devices) for i in range(devices)])


def adagrad(param, accum, grad):
    accum = accum + grad * grad
    return (param - learn_rate * grad * lax.rsqrt(accum + tiny_eps), accum)


def group_sum(term):
    if lax.axis_size("grp") == 2:
        return term.astype(jnp.float32) + shifted(term, "grp", 1).astype(jnp.float32)
    return lax.psum(term, "grp").astype(jnp.float32)


def local(ratings, user_factors, user_accum, item_factors, item_accum):
    users = user_factors
    user_acc = user_accum
    size = item_factors.shape[0] // CHUNKS
    items = [item_factors[c * size : (c + 1) * size] for c in range(CHUNKS)]
    item_acc = [item_accum[c * size : (c + 1) * size] for c in range(CHUNKS)]
    for sub_epoch in range(SUB):
        if sub_epoch > 0:
            for c in range(CHUNKS):
                items[c] = shifted(items[c].astype(jnp.bfloat16), "loop", 1).astype(jnp.float32)
                item_acc[c] = shifted(item_acc[c].astype(jnp.bfloat16), "loop", 1).astype(jnp.float32)
        for inner_step in range(INNER):
            user_half = users.astype(jnp.bfloat16)
            grad_user = shrink * users
            sums = []
            for c in range(CHUNKS):
                rate = ratings[sub_epoch, :, c * size : (c + 1) * size]
                item_half = items[c].astype(jnp.bfloat16)
                predicted = lax.dot_general(
                    user_half, item_half, (((1,), (1,)), ((), ())), preferred_element_type=jnp.float32
                )
                rate = rate.astype(jnp.float32)
                resid = jnp.where(jnp.abs(rate) > 0.25, rate - predicted, 0.0).astype(jnp.bfloat16)
                term = -lax.dot_general(
                    resid, user_half, (((0,), (0,)), ((), ())), preferred_element_type=jnp.float32
                )
                sums.append(group_sum(term.astype(jnp.bfloat16)))
                grad_user = grad_user - jnp.dot(resid, item_half, preferred_element_type=jnp.float32)
            users, user_acc = adagrad(users, user_acc, grad_user)
            for c in range(CHUNKS):
                grad_item = sums[c] + shrink * items[c]
                items[c], item_acc[c] = adagrad(items[c], item_acc[c], grad_item)
    return (users, jnp.concatenate(items, axis=0))


def solution(mesh):
    in_specs = (
        P(None, ("loop", "grp"), None),
        P(("loop", "grp"), None),
        P(("loop", "grp"), None),
        P("loop", None),
        P("loop", None),
    )
    out_specs = (P(("loop", "grp"), None), P("loop", None))
    return jax.shard_map(local, mesh=mesh, in_specs=in_specs, out_specs=out_specs, check_vma=False)
```

```python
import jax
import jax.numpy as jnp
from jax import lax
from jax.sharding import PartitionSpec as P

SUB = 2
INNER = 2
CHUNKS = 2


shrink = 0.05
learn_rate = 0.2
tiny_eps = 1e-06


def moved(shard, loop_by, grp_by):
    loops, groups = lax.axis_size("loop"), lax.axis_size("grp")
    pairs = [
        (w * groups + g, (w + loop_by) % loops * groups + (g + grp_by) % groups)
        for w in range(loops)
        for g in range(groups)
    ]
    return lax.ppermute(shard, ("loop", "grp"), pairs)


def adagrad(param, accum, grad):
    accum = accum + grad * grad
    return (param - learn_rate * grad * lax.rsqrt(accum + tiny_eps), accum)


def group_terms(term, loop_by):
    if lax.axis_size("grp") == 2:
        own = moved(term, loop_by, 0) if loop_by else term
        return (own, moved(term, loop_by, 1))
    total = lax.psum(term, "grp")
    return (moved(total, loop_by, 0) if loop_by else total,)


def item_step(items, item_acc, terms):
    items, item_acc, terms = lax.optimization_barrier((items, item_acc, terms))
    grad = sum(term.astype(jnp.float32) for term in terms) + shrink * items.astype(jnp.float32)
    return adagrad(items.astype(jnp.float32), item_acc.astype(jnp.float32), grad)


def local(ratings, user_factors, user_accum, item_factors, item_accum):
    users = user_factors
    user_acc = user_accum
    size = item_factors.shape[0] // CHUNKS
    rows = [slice(c * size, (c + 1) * size) for c in range(CHUNKS)]
    items = [item_factors[r] for r in rows]
    item_acc = [item_accum[r] for r in rows]
    terms = [None] * CHUNKS
    for step in range(SUB * INNER):
        sub_epoch = step // INNER
        last_inner = step % INNER == INNER - 1
        rotates = sub_epoch < SUB - 1
        user_half = users.astype(jnp.bfloat16)
        grad_user = shrink * users
        sent = [None] * CHUNKS
        for c in range(CHUNKS):
            if terms[c] is not None:
                items[c], item_acc[c] = item_step(items[c], item_acc[c], terms[c])
            if rotates and last_inner:
                both = jnp.concatenate((items[c], item_acc[c]), axis=0).astype(jnp.bfloat16)
                sent[c] = moved(both, 1, 0)
            rate = ratings[sub_epoch, :, rows[c]].astype(jnp.float32)
            item_half = items[c].astype(jnp.bfloat16)
            predicted = lax.dot_general(
                user_half, item_half, (((1,), (1,)), ((), ())), preferred_element_type=jnp.float32
            )
            resid = jnp.where(jnp.abs(rate) > 0.25, rate - predicted, 0.0).astype(jnp.bfloat16)
            term = -lax.dot_general(
                resid, user_half, (((0,), (0,)), ((), ())), preferred_element_type=jnp.float32
            )
            terms[c] = group_terms(term.astype(jnp.bfloat16), 1 if rotates and last_inner else 0)
            grad_user = grad_user - jnp.dot(resid, item_half, preferred_element_type=jnp.float32)
        users, user_acc = adagrad(users, user_acc, grad_user)
        if rotates and last_inner:
            items = [both[:size] for both in sent]
            item_acc = [both[size:] for both in sent]
    for c in range(CHUNKS):
        items[c], _ = item_step(items[c], item_acc[c], terms[c])
    return (users, jnp.concatenate(items, axis=0))


def solution(mesh):
    in_specs = (
        P(None, ("loop", "grp"), None),
        P(("loop", "grp"), None),
        P(("loop", "grp"), None),
        P("loop", None),
        P("loop", None),
    )
    out_specs = (P(("loop", "grp"), None), P("loop", None))
    return jax.shard_map(local, mesh=mesh, in_specs=in_specs, out_specs=out_specs, check_vma=False)
```

```python
import functools

import jax
import jax.numpy as jnp
from jax import lax
from jax.experimental import pallas as pl
from jax.experimental.pallas import tpu as pltpu
from jax.sharding import PartitionSpec as P

SUB = 2
INNER = 2
CHUNKS = 2
TILE = 256


shrink = 0.05
learn_rate = 0.2
tiny_eps = 1e-06


def moved(shard, loop_by, grp_by):
    loops, groups = lax.axis_size("loop"), lax.axis_size("grp")
    pairs = [
        (w * groups + g, (w + loop_by) % loops * groups + (g + grp_by) % groups)
        for w in range(loops)
        for g in range(groups)
    ]
    return lax.ppermute(shard, ("loop", "grp"), pairs)


def adagrad(param, accum, grad):
    accum = accum + grad * grad
    return (param - learn_rate * grad * lax.rsqrt(accum + tiny_eps), accum)


def group_terms(term):
    if lax.axis_size("grp") == 2:
        return (term, moved(term, 0, 1))
    return (lax.psum(term, "grp"),)


def item_step(items, accum, terms):
    items = items.astype(jnp.float32)
    grad = sum(term.astype(jnp.float32) for term in terms) + shrink * items
    return adagrad(items, accum.astype(jnp.float32), grad)


def chunk_kernel(n_terms, sub_epoch, column, offset, rate_ref, half_ref, grad_ref, items_ref, *refs):
    if n_terms:
        accum_ref, *refs = refs
    term_refs, (term_out, grad_out, *updated) = refs[:n_terms], refs[n_terms:]
    half = half_ref[...]
    grad = grad_ref[...]
    for start in range(0, term_out.shape[0], TILE):
        at = pl.ds(start, TILE)
        held = pl.ds(offset + start, TILE)
        items = items_ref[held, :]
        if n_terms:
            items, accum = item_step(items, accum_ref[held, :], [ref[at, :] for ref in term_refs])
            updated[0][at, :] = items
            updated[1][at, :] = accum
        item_half = items.astype(jnp.bfloat16)
        predicted = lax.dot_general(
            half, item_half, (((1,), (1,)), ((), ())), preferred_element_type=jnp.float32
        )
        rate = rate_ref[sub_epoch, :, pl.ds(column + start, TILE)].astype(jnp.float32)
        resid = jnp.where(jnp.abs(rate) > 0.25, rate - predicted, 0.0).astype(jnp.bfloat16)
        term = lax.dot_general(
            resid, half, (((0,), (0,)), ((), ())), preferred_element_type=jnp.float32
        )
        term_out[at, :] = (-term).astype(jnp.bfloat16)
        grad = grad - jnp.dot(resid, item_half, preferred_element_type=jnp.float32)
    grad_out[...] = grad


def chunk_pass(ratings, sub_epoch, rows, half, grad, items, accum, terms):
    size, rank = rows.stop - rows.start, items.shape[1]
    offset = 0 if items.shape[0] == size else rows.start
    whole = pl.BlockSpec(memory_space=pltpu.VMEM)
    out_shape = [
        jax.ShapeDtypeStruct((size, rank), jnp.bfloat16),
        jax.ShapeDtypeStruct(grad.shape, jnp.float32),
    ]
    operands = [ratings, half, grad, items]
    if terms:
        out_shape += [jax.ShapeDtypeStruct((size, rank), jnp.float32)] * 2
        operands += [accum, *terms]
    return pl.pallas_call(
        functools.partial(chunk_kernel, len(terms), sub_epoch, rows.start, offset),
        out_shape=out_shape,
        in_specs=[whole] * len(operands),
        out_specs=[whole] * len(out_shape),
        compiler_params=pltpu.CompilerParams(vmem_limit_bytes=16 * 2**20),
        cost_estimate=pl.CostEstimate(
            flops=6 * half.shape[0] * size * rank, bytes_accessed=2 * half.shape[0] * size, transcendentals=0
        ),
    )(*operands)


def last_kernel(n_terms, items_ref, accum_ref, *refs):
    items, _ = item_step(items_ref[...], accum_ref[...], [ref[...] for ref in refs[:n_terms]])
    refs[-1][...] = items


def last_item_step(rows, n_items, items, accum, terms, filled):
    size, rank = items.shape
    block = pl.BlockSpec((TILE, rank), lambda i: (i, 0))
    first = rows.start // TILE
    held = [] if filled is None else [filled]
    return pl.pallas_call(
        functools.partial(last_kernel, len(terms)),
        grid=(size // TILE,),
        out_shape=jax.ShapeDtypeStruct((n_items, rank), jnp.float32),
        in_specs=[block] * (2 + len(terms)) + [pl.BlockSpec(memory_space=pl.ANY)] * len(held),
        out_specs=pl.BlockSpec((TILE, rank), lambda i: (first + i, 0)),
        input_output_aliases={2 + len(terms): 0} if held else {},
        compiler_params=pltpu.CompilerParams(vmem_limit_bytes=16 * 2**20),
        cost_estimate=pl.CostEstimate(flops=10 * size * rank, bytes_accessed=16 * size * rank, transcendentals=0),
    )(items, accum, *terms, *held)


def local(ratings, user_factors, user_accum, item_factors, item_accum):
    users = user_factors
    user_acc = user_accum
    size = item_factors.shape[0] // CHUNKS
    rows = [slice(c * size, (c + 1) * size) for c in range(CHUNKS)]
    items = [item_factors] * CHUNKS
    item_acc = [item_accum] * CHUNKS
    terms = [()] * CHUNKS
    for step in range(SUB * INNER):
        sub_epoch = step // INNER
        if step > 0 and step % INNER == 0:
            for c in range(CHUNKS):
                stepped, accum = item_step(items[c], item_acc[c], terms[c])
                items[c] = moved(stepped.astype(jnp.bfloat16), 1, 0)
                item_acc[c] = moved(accum.astype(jnp.bfloat16), 1, 0)
                terms[c] = ()
        user_half = users.astype(jnp.bfloat16)
        grad_user = shrink * users
        for c in range(CHUNKS):
            term, grad_user, *updated = chunk_pass(
                ratings, sub_epoch, rows[c], user_half, grad_user, items[c], item_acc[c], terms[c]
            )
            if updated:
                items[c], item_acc[c] = updated
            terms[c] = group_terms(term)
        users, user_acc = adagrad(users, user_acc, grad_user)
    filled = None
    for c in range(CHUNKS):
        filled = last_item_step(rows[c], item_factors.shape[0], items[c], item_acc[c], terms[c], filled)
    return (users, filled)


def solution(mesh):
    in_specs = (
        P(None, ("loop", "grp"), None),
        P(("loop", "grp"), None),
        P(("loop", "grp"), None),
        P("loop", None),
        P("loop", None),
    )
    out_specs = (P(("loop", "grp"), None), P("loop", None))
    return jax.shard_map(local, mesh=mesh, in_specs=in_specs, out_specs=out_specs, check_vma=False)
```

```python
import functools

import jax
import jax.numpy as jnp
from jax import lax
from jax.experimental import pallas as pl
from jax.experimental.pallas import tpu as pltpu
from jax.sharding import PartitionSpec as P

SUB = 2
INNER = 2
CHUNKS = 2
TILE = 256


shrink = 0.05
learn_rate = 0.2
tiny_eps = 1e-06


def moved(shard, loop_by, grp_by):
    loops, groups = lax.axis_size("loop"), lax.axis_size("grp")
    pairs = [
        (w * groups + g, (w + loop_by) % loops * groups + (g + grp_by) % groups)
        for w in range(loops)
        for g in range(groups)
    ]
    return lax.ppermute(shard, ("loop", "grp"), pairs)


def adagrad(param, accum, grad):
    accum = accum + grad * grad
    return (param - learn_rate * grad * lax.rsqrt(accum + tiny_eps), accum)


def group_terms(term):
    if lax.axis_size("grp") == 2:
        return (term, moved(term, 0, 1))
    return (lax.psum(term, "grp"),)


def item_step(items, accum, terms):
    items = items.astype(jnp.float32)
    grad = sum(term.astype(jnp.float32) for term in terms) + shrink * items
    return adagrad(items, accum.astype(jnp.float32), grad)


def chunk_tile(half, items, rate):
    item_half = items.astype(jnp.bfloat16)
    predicted = lax.dot_general(
        half, item_half, (((1,), (1,)), ((), ())), preferred_element_type=jnp.float32
    )
    rate = rate.astype(jnp.float32)
    resid = jnp.where(jnp.abs(rate) > 0.25, rate - predicted, 0.0).astype(jnp.bfloat16)
    term = lax.dot_general(resid, half, (((0,), (0,)), ((), ())), preferred_element_type=jnp.float32)
    return (-term).astype(jnp.bfloat16), jnp.dot(resid, item_half, preferred_element_type=jnp.float32)


def params(mib=16):
    return pltpu.CompilerParams(vmem_limit_bytes=mib * 2**20)


def cost(users, items, rank):
    return pl.CostEstimate(
        flops=6 * users * items * rank, bytes_accessed=2 * users * items, transcendentals=0
    )


WHOLE = pl.BlockSpec(memory_space=pltpu.VMEM)
AWAY = pl.BlockSpec(memory_space=pltpu.HBM)


def first_kernel(column, first, rate_hbm, items_hbm, *refs):
    if first:
        users_hbm, term_out, grad_out, users_ref, rate_ref, items_ref, sems = refs
        load_users = pltpu.make_async_copy(users_hbm, users_ref, sems.at[2, 0])
        load_users.start()
    else:
        users_ref, grad_ref, term_out, grad_out, rate_ref, items_ref, sems = refs
    tiles = range(term_out.shape[0] // TILE)
    loads = []
    for t in tiles:
        at = pl.ds(column + t * TILE, TILE)
        loads.append(
            (
                pltpu.make_async_copy(items_hbm.at[at, :], items_ref.at[t], sems.at[0, t]),
                pltpu.make_async_copy(rate_hbm.at[0, :, at], rate_ref.at[t], sems.at[1, t]),
            )
        )
        for load in loads[-1]:
            load.start()
    if first:
        load_users.wait()
        grad = shrink * users_ref[...]
    else:
        grad = grad_ref[...]
    half = users_ref[...].astype(jnp.bfloat16)
    for t in tiles:
        for load in loads[t]:
            load.wait()
        term, part = chunk_tile(half, items_ref[t], rate_ref[t])
        term_out[pl.ds(t * TILE, TILE), :] = term
        grad = grad - part
    grad_out[...] = grad


def first_pass(ratings, rows, users, grad, items):
    size, (n_users, rank) = rows.stop - rows.start, users.shape
    first = grad is None
    return pl.pallas_call(
        functools.partial(first_kernel, rows.start, first),
        out_shape=[
            jax.ShapeDtypeStruct((size, rank), jnp.bfloat16),
            jax.ShapeDtypeStruct(users.shape, jnp.float32),
        ],
        in_specs=[AWAY, AWAY, AWAY] if first else [AWAY, AWAY, WHOLE, WHOLE],
        out_specs=[WHOLE] * 2,
        scratch_shapes=([pltpu.VMEM(users.shape, jnp.float32)] if first else [])
        + [
            pltpu.VMEM((size // TILE, n_users, TILE), jnp.bfloat16),
            pltpu.VMEM((size // TILE, TILE, rank), jnp.float32),
            pltpu.SemaphoreType.DMA((3, size // TILE)),
        ],
        compiler_params=params(62 if first else 16),
        cost_estimate=cost(n_users, size, rank),
    )(ratings, items, users, *([] if first else [grad]))


def chunk_kernel(n_terms, sub_epoch, column, offset, rate_ref, half_ref, grad_ref, items_ref, *refs):
    if n_terms:
        accum_ref, *refs = refs
    term_refs, (term_out, grad_out, *updated) = refs[:n_terms], refs[n_terms:]
    half = half_ref[...]
    grad = grad_ref[...]
    for start in range(0, term_out.shape[0], TILE):
        at = pl.ds(start, TILE)
        held = pl.ds(offset + start, TILE)
        items = items_ref[held, :]
        if n_terms:
            items, accum = item_step(items, accum_ref[held, :], [ref[at, :] for ref in term_refs])
            updated[0][at, :] = items
            updated[1][at, :] = accum
        term_out[at, :], part = chunk_tile(half, items, rate_ref[sub_epoch, :, pl.ds(column + start, TILE)])
        grad = grad - part
    grad_out[...] = grad


def chunk_pass(ratings, sub_epoch, rows, half, grad, items, accum, terms):
    size, rank = rows.stop - rows.start, items.shape[1]
    offset = 0 if items.shape[0] == size else rows.start
    out_shape = [
        jax.ShapeDtypeStruct((size, rank), jnp.bfloat16),
        jax.ShapeDtypeStruct(grad.shape, jnp.float32),
    ]
    operands = [ratings, half, grad, items]
    if terms:
        out_shape += [jax.ShapeDtypeStruct((size, rank), jnp.float32)] * 2
        operands += [accum, *terms]
    return pl.pallas_call(
        functools.partial(chunk_kernel, len(terms), sub_epoch, rows.start, offset),
        out_shape=out_shape,
        in_specs=[WHOLE] * len(operands),
        out_specs=[WHOLE] * len(out_shape),
        compiler_params=params(),
        cost_estimate=cost(half.shape[0], size, rank),
    )(*operands)


def parting_kernel(n_terms, items_ref, accum_ref, *refs):
    items, accum = item_step(items_ref[...], accum_ref[...], [ref[...] for ref in refs[:n_terms]])
    items_out, accum_out = refs[-2:]
    items_out[...] = items.astype(jnp.bfloat16)
    accum_out[...] = accum.astype(jnp.bfloat16)


def parting_step(items, accum, terms, before):
    return pl.pallas_call(
        functools.partial(parting_kernel, len(terms)),
        out_shape=[jax.ShapeDtypeStruct(items.shape, jnp.bfloat16)] * 2,
        in_specs=[WHOLE] * (2 + len(terms)) + [pl.BlockSpec(memory_space=pl.ANY)] * len(before),
        out_specs=[WHOLE] * 2,
        compiler_params=params(),
        cost_estimate=cost(1, *items.shape),
    )(items, accum, *terms, *before)


def last_kernel(n_terms, row, items_ref, accum_ref, *refs):
    out_hbm, out_ref, sems = refs[-3:]
    stores = []
    for t in range(items_ref.shape[0] // TILE):
        at = pl.ds(t * TILE, TILE)
        out_ref[at, :], _ = item_step(items_ref[at, :], accum_ref[at, :], [ref[at, :] for ref in refs[:n_terms]])
        stores.append(
            pltpu.make_async_copy(out_ref.at[at, :], out_hbm.at[pl.ds(row + t * TILE, TILE), :], sems.at[t])
        )
        stores[-1].start()
    for store in stores:
        store.wait()


def last_item_step(rows, n_items, items, accum, terms, filled):
    size, rank = items.shape
    return pl.pallas_call(
        functools.partial(last_kernel, len(terms), rows.start),
        out_shape=jax.ShapeDtypeStruct((n_items, rank), jnp.float32),
        in_specs=[WHOLE] * (2 + len(terms)) + [AWAY] * len(filled),
        out_specs=AWAY,
        scratch_shapes=[
            pltpu.VMEM((size, rank), jnp.float32),
            pltpu.SemaphoreType.DMA((size // TILE,)),
        ],
        input_output_aliases={2 + len(terms): 0} if filled else {},
        compiler_params=params(),
        cost_estimate=cost(1, size, rank),
    )(items, accum, *terms, *filled)


def local(ratings, user_factors, user_accum, item_factors, item_accum):
    users = user_factors
    user_acc = user_accum
    size = item_factors.shape[0] // CHUNKS
    rows = [slice(c * size, (c + 1) * size) for c in range(CHUNKS)]
    items = [item_factors] * CHUNKS
    item_acc = [item_accum] * CHUNKS
    terms = [()] * CHUNKS
    for step in range(SUB * INNER):
        sub_epoch = step // INNER
        if step > 0 and step % INNER == 0:
            before = []
            for c in range(CHUNKS):
                stepped, accum = parting_step(items[c], item_acc[c], terms[c], before)
                items[c] = moved(stepped, 1, 0)
                item_acc[c] = moved(accum, 1, 0)
                terms[c] = ()
                before = [stepped]
        if step == 0:
            grad_user = None
        else:
            user_half = users.astype(jnp.bfloat16)
            grad_user = shrink * users
        for c in range(CHUNKS):
            if step == 0:
                term, grad_user = first_pass(ratings, rows[c], users, grad_user, items[c])
            else:
                term, grad_user, *updated = chunk_pass(
                    ratings, sub_epoch, rows[c], user_half, grad_user, items[c], item_acc[c], terms[c]
                )
                if updated:
                    items[c], item_acc[c] = updated
            terms[c] = group_terms(term)
        users, user_acc = adagrad(users, user_acc, grad_user)
    filled = []
    for c in range(CHUNKS):
        filled = [last_item_step(rows[c], item_factors.shape[0], items[c], item_acc[c], terms[c], filled)]
    return (users, filled[0])


def solution(mesh):
    in_specs = (
        P(None, ("loop", "grp"), None),
        P(("loop", "grp"), None),
        P(("loop", "grp"), None),
        P("loop", None),
        P("loop", None),
    )
    out_specs = (P(("loop", "grp"), None), P("loop", None))
    return jax.shard_map(local, mesh=mesh, in_specs=in_specs, out_specs=out_specs, check_vma=False)
```

```python
import functools

import jax
import jax.numpy as jnp
from jax import lax
from jax.experimental import pallas as pl
from jax.experimental.pallas import tpu as pltpu
from jax.sharding import PartitionSpec as P

SUB = 2
INNER = 2
CHUNKS = 2
EARLY = 1
TILE = 256


shrink = 0.05
learn_rate = 0.2
tiny_eps = 1e-06


def moved(shard, loop_by, grp_by):
    loops, groups = lax.axis_size("loop"), lax.axis_size("grp")
    pairs = [
        (w * groups + g, (w + loop_by) % loops * groups + (g + grp_by) % groups)
        for w in range(loops)
        for g in range(groups)
    ]
    return lax.ppermute(shard, ("loop", "grp"), pairs)


def adagrad(param, accum, grad):
    accum = accum + grad * grad
    return (param - learn_rate * grad * lax.rsqrt(accum + tiny_eps), accum)


def group_terms(term, loop_by=0):
    if lax.axis_size("grp") == 2:
        own = moved(term, loop_by, 0) if loop_by else term
        return (own, moved(term, loop_by, 1))
    total = lax.psum(term, "grp")
    return (moved(total, loop_by, 0) if loop_by else total,)


def item_step(items, accum, terms):
    items = items.astype(jnp.float32)
    grad = sum(term.astype(jnp.float32) for term in terms) + shrink * items
    return adagrad(items, accum.astype(jnp.float32), grad)


def chunk_tile(half, half_t, items, rate):
    item_half = items.astype(jnp.bfloat16)
    predicted = lax.dot_general(
        half, item_half, (((1,), (1,)), ((), ())), preferred_element_type=jnp.float32
    )
    rate = rate.astype(jnp.float32)
    resid = jnp.where(jnp.abs(rate) > 0.25, rate - predicted, 0.0).astype(jnp.bfloat16)
    term = jnp.dot(half_t, resid, preferred_element_type=jnp.float32)
    return (-term).T.astype(jnp.bfloat16), jnp.dot(resid, item_half, preferred_element_type=jnp.float32)


def params(mib=16):
    return pltpu.CompilerParams(vmem_limit_bytes=mib * 2**20)


def cost(users, items, rank):
    return pl.CostEstimate(
        flops=6 * users * items * rank, bytes_accessed=2 * users * items, transcendentals=0
    )


WHOLE = pl.BlockSpec(memory_space=pltpu.VMEM)
AWAY = pl.BlockSpec(memory_space=pltpu.HBM)


def first_kernel(column, rate_hbm, items_hbm, users_hbm, term_out, grad_out, half_out, *scratch):
    users_ref, rate_ref, items_ref, sems = scratch
    load_users = pltpu.make_async_copy(users_hbm, users_ref, sems.at[2, 0])
    load_users.start()
    tiles = range(term_out.shape[0] // TILE)
    loads = []
    for t in tiles:
        at = pl.ds(column + t * TILE, TILE)
        loads.append(
            (
                pltpu.make_async_copy(items_hbm.at[at, :], items_ref.at[t], sems.at[0, t]),
                pltpu.make_async_copy(rate_hbm.at[0, :, at], rate_ref.at[t], sems.at[1, t]),
            )
        )
        for load in loads[-1]:
            load.start()
    load_users.wait()
    grad = shrink * users_ref[...]
    half = users_ref[...].astype(jnp.bfloat16)
    half_t = half.T
    half_out[...] = half
    for t in tiles:
        for load in loads[t]:
            load.wait()
        term, part = chunk_tile(half, half_t, items_ref[t], rate_ref[t])
        term_out[pl.ds(t * TILE, TILE), :] = term
        grad = grad - part
    grad_out[...] = grad


def first_pass(ratings, rows, users, items):
    size, (n_users, rank) = rows.stop - rows.start, users.shape
    return pl.pallas_call(
        functools.partial(first_kernel, rows.start),
        out_shape=[
            jax.ShapeDtypeStruct((size, rank), jnp.bfloat16),
            jax.ShapeDtypeStruct(users.shape, jnp.float32),
            jax.ShapeDtypeStruct(users.shape, jnp.bfloat16),
        ],
        in_specs=[AWAY] * 3,
        out_specs=[WHOLE] * 3,
        scratch_shapes=[
            pltpu.VMEM(users.shape, jnp.float32),
            pltpu.VMEM((size // TILE, n_users, TILE), jnp.bfloat16),
            pltpu.VMEM((size // TILE, TILE, rank), jnp.float32),
            pltpu.SemaphoreType.DMA((3, size // TILE)),
        ],
        compiler_params=params(62),
        cost_estimate=cost(n_users, size, rank),
    )(ratings, items, users)


def chunk_kernel(n_terms, sub_epoch, column, offset, rate_ref, half_ref, grad_ref, items_ref, *refs):
    if n_terms:
        accum_ref, *refs = refs
    term_refs, (term_out, grad_out, *updated) = refs[:n_terms], refs[n_terms:]
    half = half_ref[...]
    half_t = half.T
    grad = grad_ref[...]
    for start in range(0, term_out.shape[0], TILE):
        at = pl.ds(start, TILE)
        held = pl.ds(offset + start, TILE)
        items = items_ref[held, :]
        if n_terms:
            items, accum = item_step(items, accum_ref[held, :], [ref[at, :] for ref in term_refs])
            updated[0][at, :] = items.astype(updated[0].dtype)
            updated[1][at, :] = accum.astype(updated[1].dtype)
        term_out[at, :], part = chunk_tile(half, half_t, items, rate_ref[sub_epoch, :, pl.ds(column + start, TILE)])
        grad = grad - part
    grad_out[...] = grad


def chunk_pass(ratings, sub_epoch, rows, half, grad, items, accum, terms, kept):
    size, rank = rows.stop - rows.start, items.shape[1]
    offset = 0 if items.shape[0] == size else rows.start
    out_shape = [
        jax.ShapeDtypeStruct((size, rank), jnp.bfloat16),
        jax.ShapeDtypeStruct(grad.shape, jnp.float32),
    ]
    operands = [ratings, half, grad, items]
    if terms:
        out_shape += [jax.ShapeDtypeStruct((size, rank), kept)] * 2
        operands += [accum, *terms]
    return pl.pallas_call(
        functools.partial(chunk_kernel, len(terms), sub_epoch, rows.start, offset),
        out_shape=out_shape,
        in_specs=[WHOLE] * len(operands),
        out_specs=[WHOLE] * len(out_shape),
        compiler_params=params(),
        cost_estimate=cost(half.shape[0], size, rank),
    )(*operands)


def parting_kernel(n_terms, items_ref, accum_ref, *refs):
    items, accum = item_step(items_ref[...], accum_ref[...], [ref[...] for ref in refs[:n_terms]])
    items_out, accum_out = refs[-2:]
    items_out[...] = items.astype(items_out.dtype)
    accum_out[...] = accum.astype(accum_out.dtype)


def parting_step(items, accum, terms, before):
    return pl.pallas_call(
        functools.partial(parting_kernel, len(terms)),
        out_shape=[jax.ShapeDtypeStruct(items.shape, jnp.bfloat16)] * 2,
        in_specs=[WHOLE] * (2 + len(terms)) + [pl.BlockSpec(memory_space=pl.ANY)] * len(before),
        out_specs=[WHOLE] * 2,
        compiler_params=params(),
        cost_estimate=cost(1, *items.shape),
    )(items, accum, *terms, *before)


def last_kernel(n_terms, row, items_ref, accum_ref, *refs):
    out_hbm, out_ref, sems = refs[-3:]
    stores = []
    for t in range(items_ref.shape[0] // TILE):
        at = pl.ds(t * TILE, TILE)
        out_ref[at, :], _ = item_step(items_ref[at, :], accum_ref[at, :], [ref[at, :] for ref in refs[:n_terms]])
        stores.append(
            pltpu.make_async_copy(out_ref.at[at, :], out_hbm.at[pl.ds(row + t * TILE, TILE), :], sems.at[t])
        )
        stores[-1].start()
    for store in stores:
        store.wait()


def last_item_step(rows, n_items, items, accum, terms, filled):
    size, rank = items.shape
    return pl.pallas_call(
        functools.partial(last_kernel, len(terms), rows.start),
        out_shape=jax.ShapeDtypeStruct((n_items, rank), jnp.float32),
        in_specs=[WHOLE] * (2 + len(terms)) + [AWAY] * len(filled),
        out_specs=AWAY,
        scratch_shapes=[
            pltpu.VMEM((size, rank), jnp.float32),
            pltpu.SemaphoreType.DMA((size // TILE,)),
        ],
        input_output_aliases={2 + len(terms): 0} if filled else {},
        compiler_params=params(),
        cost_estimate=cost(1, size, rank),
    )(items, accum, *terms, *filled)


def local(ratings, user_factors, user_accum, item_factors, item_accum):
    users = user_factors
    user_acc = user_accum
    size = item_factors.shape[0] // CHUNKS
    rows = [slice(c * size, (c + 1) * size) for c in range(CHUNKS)]
    items = [item_factors] * CHUNKS
    item_acc = [item_accum] * CHUNKS
    terms = [()] * CHUNKS
    for step in range(SUB * INNER):
        sub_epoch = step // INNER
        early = EARLY if step % INNER == INNER - 1 and sub_epoch < SUB - 1 else 0
        if step > 0:
            user_half = users.astype(jnp.bfloat16)
            grad_user = shrink * users
        for c in range(CHUNKS):
            if step > 0 and step % INNER == 0 and c == EARLY:
                before = [term] if c else []
                for d in range(c, CHUNKS):
                    items[d], item_acc[d] = parting_step(items[d], item_acc[d], terms[d], before)
                    before = [items[d]]
                    items[d] = moved(items[d], 1, 0)
                    item_acc[d] = moved(item_acc[d], 1, 0)
                    terms[d] = ()
            if step == 0 and c == 0:
                term, grad_user, user_half = first_pass(ratings, rows[c], users, items[c])
            else:
                kept = jnp.bfloat16 if c < early else jnp.float32
                term, grad_user, *updated = chunk_pass(
                    ratings, sub_epoch, rows[c], user_half, grad_user, items[c], item_acc[c], terms[c], kept
                )
                if updated:
                    items[c], item_acc[c] = updated
            terms[c] = group_terms(term, 1 if c < early else 0)
            if c < early:
                items[c] = moved(items[c], 1, 0)
                item_acc[c] = moved(item_acc[c], 1, 0)
        users, user_acc = adagrad(users, user_acc, grad_user)
    filled = []
    for c in range(CHUNKS):
        filled = [last_item_step(rows[c], item_factors.shape[0], items[c], item_acc[c], terms[c], filled)]
    return (users, filled[0])


def solution(mesh):
    in_specs = (
        P(None, ("loop", "grp"), None),
        P(("loop", "grp"), None),
        P(("loop", "grp"), None),
        P("loop", None),
        P("loop", None),
    )
    out_specs = (P(("loop", "grp"), None), P("loop", None))
    return jax.shard_map(local, mesh=mesh, in_specs=in_specs, out_specs=out_specs, check_vma=False)
```

```python
import functools

import jax
import jax.numpy as jnp
from jax import lax
from jax.experimental import pallas as pl
from jax.experimental.pallas import tpu as pltpu
from jax.sharding import PartitionSpec as P

SUB = 2
INNER = 2
CHUNKS = 2
TILE = 256


shrink = 0.05
learn_rate = 0.2
tiny_eps = 1e-06


def moved(shard, loop_by, grp_by):
    loops, groups = lax.axis_size("loop"), lax.axis_size("grp")
    pairs = [
        (w * groups + g, (w + loop_by) % loops * groups + (g + grp_by) % groups)
        for w in range(loops)
        for g in range(groups)
    ]
    return lax.ppermute(shard, ("loop", "grp"), pairs)


def adagrad(param, accum, grad):
    accum = accum + grad * grad
    return (param - learn_rate * grad * lax.rsqrt(accum + tiny_eps), accum)


def group_terms(term):
    if lax.axis_size("grp") == 2:
        return (term, moved(term, 0, 1))
    return (lax.psum(term, "grp"),)


def item_step(items, accum, terms):
    items = items.astype(jnp.float32)
    grad = sum(term.astype(jnp.float32) for term in terms) + shrink * items
    return adagrad(items, accum.astype(jnp.float32), grad)


def chunk_tile(half, half_t, items, rate):
    item_half = items.astype(jnp.bfloat16)
    predicted = lax.dot_general(
        half, item_half, (((1,), (1,)), ((), ())), preferred_element_type=jnp.float32
    )
    rate = rate.astype(jnp.float32)
    resid = jnp.where(jnp.abs(rate) > 0.25, rate - predicted, 0.0).astype(jnp.bfloat16)
    term = jnp.dot(half_t, resid, preferred_element_type=jnp.float32)
    return (-term).T.astype(jnp.bfloat16), jnp.dot(resid, item_half, preferred_element_type=jnp.float32)


def params(mib=16):
    return pltpu.CompilerParams(vmem_limit_bytes=mib * 2**20)


def cost(users, items, rank):
    return pl.CostEstimate(
        flops=6 * users * items * rank, bytes_accessed=2 * users * items, transcendentals=0
    )


WHOLE = pl.BlockSpec(memory_space=pltpu.VMEM)
AWAY = pl.BlockSpec(memory_space=pltpu.HBM)


def first_kernel(column, rate_hbm, items_hbm, users_hbm, term_out, grad_out, half_out, *scratch):
    users_ref, rate_ref, items_ref, sems = scratch
    load_users = pltpu.make_async_copy(users_hbm, users_ref, sems.at[2, 0])
    load_users.start()
    tiles = range(term_out.shape[0] // TILE)
    loads = []
    for t in tiles:
        at = pl.ds(column + t * TILE, TILE)
        loads.append(
            (
                pltpu.make_async_copy(items_hbm.at[at, :], items_ref.at[t], sems.at[0, t]),
                pltpu.make_async_copy(rate_hbm.at[0, :, at], rate_ref.at[t], sems.at[1, t]),
            )
        )
        for load in loads[-1]:
            load.start()
    load_users.wait()
    grad = shrink * users_ref[...]
    half = users_ref[...].astype(jnp.bfloat16)
    half_t = half.T
    half_out[...] = half
    for t in tiles:
        for load in loads[t]:
            load.wait()
        term, part = chunk_tile(half, half_t, items_ref[t], rate_ref[t])
        term_out[pl.ds(t * TILE, TILE), :] = term
        grad = grad - part
    grad_out[...] = grad


def first_pass(ratings, rows, users, items):
    size, (n_users, rank) = rows.stop - rows.start, users.shape
    return pl.pallas_call(
        functools.partial(first_kernel, rows.start),
        out_shape=[
            jax.ShapeDtypeStruct((size, rank), jnp.bfloat16),
            jax.ShapeDtypeStruct(users.shape, jnp.float32),
            jax.ShapeDtypeStruct(users.shape, jnp.bfloat16),
        ],
        in_specs=[AWAY] * 3,
        out_specs=[WHOLE] * 3,
        scratch_shapes=[
            pltpu.VMEM(users.shape, jnp.float32),
            pltpu.VMEM((size // TILE, n_users, TILE), jnp.bfloat16),
            pltpu.VMEM((size // TILE, TILE, rank), jnp.float32),
            pltpu.SemaphoreType.DMA((3, size // TILE)),
        ],
        compiler_params=params(62),
        cost_estimate=cost(n_users, size, rank),
    )(ratings, items, users)


def chunk_kernel(n_terms, leaves, sub_epoch, column, offset, rate_ref, half_ref, grad_ref, items_ref, *refs):
    if n_terms:
        accum_ref, *refs = refs
    if leaves:
        leaving_ref, *refs, leaving_out = refs
        leaving_out[...] = leaving_ref[...]
    term_refs, (term_out, grad_out, *updated) = refs[:n_terms], refs[n_terms:]
    half = half_ref[...]
    half_t = half.T
    grad = grad_ref[...]
    for start in range(0, term_out.shape[0], TILE):
        at = pl.ds(start, TILE)
        held = pl.ds(offset + start, TILE)
        items = items_ref[held, :]
        if n_terms:
            items, accum = item_step(items, accum_ref[held, :], [ref[at, :] for ref in term_refs])
            updated[0][at, :] = items
            updated[1][at, :] = accum
        term_out[at, :], part = chunk_tile(half, half_t, items, rate_ref[sub_epoch, :, pl.ds(column + start, TILE)])
        grad = grad - part
    grad_out[...] = grad


def chunk_pass(ratings, sub_epoch, rows, half, grad, items, accum, terms, leaving=()):
    size, rank = rows.stop - rows.start, items.shape[1]
    offset = 0 if items.shape[0] == size else rows.start
    out_shape = [
        jax.ShapeDtypeStruct((size, rank), jnp.bfloat16),
        jax.ShapeDtypeStruct(grad.shape, jnp.float32),
    ]
    operands = [ratings, half, grad, items]
    if terms:
        out_shape += [jax.ShapeDtypeStruct((size, rank), jnp.float32)] * 2
        operands += [accum, *terms]
    operands += leaving
    out_shape += [jax.ShapeDtypeStruct(array.shape, array.dtype) for array in leaving]
    return pl.pallas_call(
        functools.partial(chunk_kernel, len(terms), len(leaving), sub_epoch, rows.start, offset),
        out_shape=out_shape,
        in_specs=[WHOLE] * len(operands),
        out_specs=[WHOLE] * len(out_shape),
        compiler_params=params(),
        cost_estimate=cost(half.shape[0], size, rank),
    )(*operands)


def parting_kernel(n_terms, items_ref, accum_ref, *refs):
    items, accum = item_step(items_ref[...], accum_ref[...], [ref[...] for ref in refs[:n_terms]])
    items_out, accum_out = refs[-2:]
    items_out[...] = items.astype(items_out.dtype)
    accum_out[...] = accum.astype(accum_out.dtype)


def parting_step(items, accum, terms, before):
    return pl.pallas_call(
        functools.partial(parting_kernel, len(terms)),
        out_shape=[jax.ShapeDtypeStruct(items.shape, jnp.bfloat16)] * 2,
        in_specs=[WHOLE] * (2 + len(terms)) + [pl.BlockSpec(memory_space=pl.ANY)] * len(before),
        out_specs=[WHOLE] * 2,
        compiler_params=params(),
        cost_estimate=cost(1, *items.shape),
    )(items, accum, *terms, *before)


def last_kernel(n_terms, row, items_ref, accum_ref, *refs):
    out_hbm, out_ref, sems = refs[-3:]
    stores = []
    for t in range(items_ref.shape[0] // TILE):
        at = pl.ds(t * TILE, TILE)
        out_ref[at, :], _ = item_step(items_ref[at, :], accum_ref[at, :], [ref[at, :] for ref in refs[:n_terms]])
        stores.append(
            pltpu.make_async_copy(out_ref.at[at, :], out_hbm.at[pl.ds(row + t * TILE, TILE), :], sems.at[t])
        )
        stores[-1].start()
    for store in stores:
        store.wait()


def last_item_step(rows, n_items, items, accum, terms, filled):
    size, rank = items.shape
    return pl.pallas_call(
        functools.partial(last_kernel, len(terms), rows.start),
        out_shape=jax.ShapeDtypeStruct((n_items, rank), jnp.float32),
        in_specs=[WHOLE] * (2 + len(terms)) + [AWAY] * len(filled),
        out_specs=AWAY,
        scratch_shapes=[
            pltpu.VMEM((size, rank), jnp.float32),
            pltpu.SemaphoreType.DMA((size // TILE,)),
        ],
        input_output_aliases={2 + len(terms): 0} if filled else {},
        compiler_params=params(),
        cost_estimate=cost(1, size, rank),
    )(items, accum, *terms, *filled)


def local(ratings, user_factors, user_accum, item_factors, item_accum):
    users = user_factors
    user_acc = user_accum
    size = item_factors.shape[0] // CHUNKS
    rows = [slice(c * size, (c + 1) * size) for c in range(CHUNKS)]
    items = [item_factors] * CHUNKS
    item_acc = [item_accum] * CHUNKS
    terms = [()] * CHUNKS
    for step in range(SUB * INNER):
        sub_epoch = step // INNER
        rotates = step > 0 and step % INNER == 0
        if rotates:
            before = []
            for c in range(CHUNKS):
                items[c], item_acc[c] = parting_step(items[c], item_acc[c], terms[c], before)
                before = [items[c]]
                items[c] = moved(items[c], 1, 0)
                terms[c] = ()
        if step > 0:
            user_half = users.astype(jnp.bfloat16)
            grad_user = shrink * users
        for c in range(CHUNKS):
            if step == 0 and c == 0:
                term, grad_user, user_half = first_pass(ratings, rows[c], users, items[c])
            else:
                term, grad_user, *updated = chunk_pass(
                    ratings, sub_epoch, rows[c], user_half, grad_user, items[c], item_acc[c], terms[c],
                    [item_acc[c]] if rotates else [],
                )
                if rotates:
                    item_acc[c] = moved(updated[0], 1, 0)
                elif updated:
                    items[c], item_acc[c] = updated
            terms[c] = group_terms(term)
        users, user_acc = adagrad(users, user_acc, grad_user)
    filled = []
    for c in range(CHUNKS):
        filled = [last_item_step(rows[c], item_factors.shape[0], items[c], item_acc[c], terms[c], filled)]
    return (users, filled[0])


def solution(mesh):
    in_specs = (
        P(None, ("loop", "grp"), None),
        P(("loop", "grp"), None),
        P(("loop", "grp"), None),
        P("loop", None),
        P("loop", None),
    )
    out_specs = (P(("loop", "grp"), None), P("loop", None))
    return jax.shard_map(local, mesh=mesh, in_specs=in_specs, out_specs=out_specs, check_vma=False)
```

```python
import functools

import jax
import jax.numpy as jnp
from jax import lax
from jax.experimental import pallas as pl
from jax.experimental.pallas import tpu as pltpu
from jax.sharding import PartitionSpec as P

SUB = 2
INNER = 2
CHUNKS = 2
TILE = 256


shrink = 0.05
learn_rate = 0.2
tiny_eps = 1e-06


def moved(shard, loop_by, grp_by):
    loops, groups = lax.axis_size("loop"), lax.axis_size("grp")
    pairs = [
        (w * groups + g, (w + loop_by) % loops * groups + (g + grp_by) % groups)
        for w in range(loops)
        for g in range(groups)
    ]
    return lax.ppermute(shard, ("loop", "grp"), pairs)


def adagrad(param, accum, grad):
    accum = accum + grad * grad
    return (param - learn_rate * grad * lax.rsqrt(accum + tiny_eps), accum)


def group_terms(term):
    if lax.axis_size("grp") == 2:
        return (term, moved(term, 0, 1))
    return (lax.psum(term, "grp"),)


def item_step(items, accum, terms):
    items = items.astype(jnp.float32)
    grad = sum(term.astype(jnp.float32) for term in terms) + shrink * items
    return adagrad(items, accum.astype(jnp.float32), grad)


def chunk_tile(half, half_t, items, rate):
    item_half = items.astype(jnp.bfloat16)
    predicted = lax.dot_general(
        half, item_half, (((1,), (1,)), ((), ())), preferred_element_type=jnp.float32
    )
    rate = rate.astype(jnp.float32)
    resid = jnp.where(jnp.abs(rate) > 0.25, rate - predicted, 0.0).astype(jnp.bfloat16)
    term = jnp.dot(half_t, resid, preferred_element_type=jnp.float32)
    return (-term).T.astype(jnp.bfloat16), jnp.dot(resid, item_half, preferred_element_type=jnp.float32)


def params(mib=16):
    return pltpu.CompilerParams(vmem_limit_bytes=mib * 2**20)


def cost(users, items, rank):
    return pl.CostEstimate(
        flops=6 * users * items * rank, bytes_accessed=2 * users * items, transcendentals=0
    )


WHOLE = pl.BlockSpec(memory_space=pltpu.VMEM)
AWAY = pl.BlockSpec(memory_space=pltpu.HBM)


def first_kernel(column, rate_hbm, items_hbm, users_hbm, term_out, grad_out, half_out, *scratch):
    users_ref, rate_ref, items_ref, sems = scratch
    load_users = pltpu.make_async_copy(users_hbm, users_ref, sems.at[2, 0])
    load_users.start()
    tiles = range(term_out.shape[0] // TILE)
    loads = []
    for t in tiles:
        at = pl.ds(column + t * TILE, TILE)
        loads.append(
            (
                pltpu.make_async_copy(items_hbm.at[at, :], items_ref.at[t], sems.at[0, t]),
                pltpu.make_async_copy(rate_hbm.at[0, :, at], rate_ref.at[t], sems.at[1, t]),
            )
        )
        for load in loads[-1]:
            load.start()
    load_users.wait()
    grad = shrink * users_ref[...]
    half = users_ref[...].astype(jnp.bfloat16)
    half_t = half.T
    half_out[...] = half
    for t in tiles:
        for load in loads[t]:
            load.wait()
        term, part = chunk_tile(half, half_t, items_ref[t], rate_ref[t])
        term_out[pl.ds(t * TILE, TILE), :] = term
        grad = grad - part
    grad_out[...] = grad


def first_pass(ratings, rows, users, items):
    size, (n_users, rank) = rows.stop - rows.start, users.shape
    return pl.pallas_call(
        functools.partial(first_kernel, rows.start),
        out_shape=[
            jax.ShapeDtypeStruct((size, rank), jnp.bfloat16),
            jax.ShapeDtypeStruct(users.shape, jnp.float32),
            jax.ShapeDtypeStruct(users.shape, jnp.bfloat16),
        ],
        in_specs=[AWAY] * 3,
        out_specs=[WHOLE] * 3,
        scratch_shapes=[
            pltpu.VMEM(users.shape, jnp.float32),
            pltpu.VMEM((size // TILE, n_users, TILE), jnp.bfloat16),
            pltpu.VMEM((size // TILE, TILE, rank), jnp.float32),
            pltpu.SemaphoreType.DMA((3, size // TILE)),
        ],
        compiler_params=params(62),
        cost_estimate=cost(n_users, size, rank),
    )(ratings, items, users)


def chunk_kernel(n_terms, leaves, sub_epoch, column, offset, rate_ref, half_ref, grad_ref, items_ref, *refs):
    if leaves:
        leaving_ref, *refs, leaving_out = refs
        leaving_out[...] = leaving_ref[...]
    term_refs, refs = refs[:n_terms], refs[n_terms:]
    if n_terms:
        accum_ref, *refs = refs
    term_out, grad_out, *updated = refs
    half = half_ref[...]
    half_t = half.T
    grad = grad_ref[...]
    for start in range(0, term_out.shape[0], TILE):
        at = pl.ds(start, TILE)
        held = pl.ds(offset + start, TILE)
        items = items_ref[held, :]
        if n_terms:
            items, accum = item_step(items, accum_ref[held, :], [ref[at, :] for ref in term_refs])
            updated[0][at, :] = items
            updated[1][at, :] = accum
        term_out[at, :], part = chunk_tile(half, half_t, items, rate_ref[sub_epoch, :, pl.ds(column + start, TILE)])
        grad = grad - part
    grad_out[...] = grad


def chunk_pass(ratings, sub_epoch, rows, half, grad, items, accum, terms, leaving=()):
    size, rank = rows.stop - rows.start, items.shape[1]
    offset = 0 if items.shape[0] == size else rows.start
    out_shape = [
        jax.ShapeDtypeStruct((size, rank), jnp.bfloat16),
        jax.ShapeDtypeStruct(grad.shape, jnp.float32),
    ]
    operands = [ratings, half, grad, items]
    if terms:
        out_shape += [jax.ShapeDtypeStruct((size, rank), jnp.float32)] * 2
        operands += [*terms, accum]
    operands += leaving
    out_shape += [jax.ShapeDtypeStruct(array.shape, array.dtype) for array in leaving]
    return pl.pallas_call(
        functools.partial(chunk_kernel, len(terms), len(leaving), sub_epoch, rows.start, offset),
        out_shape=out_shape,
        in_specs=[WHOLE] * len(operands),
        out_specs=[WHOLE] * len(out_shape),
        compiler_params=params(),
        cost_estimate=cost(half.shape[0], size, rank),
    )(*operands)


def parting_kernel(n_terms, items_ref, accum_ref, *refs):
    items, accum = item_step(items_ref[...], accum_ref[...], [ref[...] for ref in refs[:n_terms]])
    items_out, accum_out = refs[-2:]
    items_out[...] = items.astype(items_out.dtype)
    accum_out[...] = accum.astype(accum_out.dtype)


def parting_step(items, accum, terms, before):
    return pl.pallas_call(
        functools.partial(parting_kernel, len(terms)),
        out_shape=[jax.ShapeDtypeStruct(items.shape, jnp.bfloat16)] * 2,
        in_specs=[WHOLE] * (2 + len(terms)) + [pl.BlockSpec(memory_space=pl.ANY)] * len(before),
        out_specs=[WHOLE] * 2,
        compiler_params=params(),
        cost_estimate=cost(1, *items.shape),
    )(items, accum, *terms, *before)


def last_kernel(n_terms, row, items_ref, accum_ref, *refs):
    out_hbm, out_ref, sems = refs[-3:]
    stores = []
    for t in range(items_ref.shape[0] // TILE):
        at = pl.ds(t * TILE, TILE)
        out_ref[at, :], _ = item_step(items_ref[at, :], accum_ref[at, :], [ref[at, :] for ref in refs[:n_terms]])
        stores.append(
            pltpu.make_async_copy(out_ref.at[at, :], out_hbm.at[pl.ds(row + t * TILE, TILE), :], sems.at[t])
        )
        stores[-1].start()
    for store in stores:
        store.wait()


def last_item_step(rows, n_items, items, accum, terms, filled):
    size, rank = items.shape
    return pl.pallas_call(
        functools.partial(last_kernel, len(terms), rows.start),
        out_shape=jax.ShapeDtypeStruct((n_items, rank), jnp.float32),
        in_specs=[WHOLE] * (2 + len(terms)) + [AWAY] * len(filled),
        out_specs=AWAY,
        scratch_shapes=[
            pltpu.VMEM((size, rank), jnp.float32),
            pltpu.SemaphoreType.DMA((size // TILE,)),
        ],
        input_output_aliases={2 + len(terms): 0} if filled else {},
        compiler_params=params(),
        cost_estimate=cost(1, size, rank),
    )(items, accum, *terms, *filled)


def local(ratings, user_factors, user_accum, item_factors, item_accum):
    users = user_factors
    user_acc = user_accum
    size = item_factors.shape[0] // CHUNKS
    rows = [slice(c * size, (c + 1) * size) for c in range(CHUNKS)]
    items = [item_factors] * CHUNKS
    item_acc = [item_accum] * CHUNKS
    terms = [()] * CHUNKS
    for step in range(SUB * INNER):
        sub_epoch = step // INNER
        rotates = step > 0 and step % INNER == 0
        if rotates:
            before = []
            for c in range(CHUNKS):
                items[c], item_acc[c] = parting_step(items[c], item_acc[c], terms[c], before)
                before = [items[c]]
                items[c] = moved(items[c], 1, 0)
                terms[c] = ()
        if step > 0:
            user_half = users.astype(jnp.bfloat16)
            grad_user = shrink * users
        for c in range(CHUNKS):
            if step == 0 and c == 0:
                term, grad_user, user_half = first_pass(ratings, rows[c], users, items[c])
            else:
                term, grad_user, *updated = chunk_pass(
                    ratings, sub_epoch, rows[c], user_half, grad_user, items[c], item_acc[c], terms[c],
                    [item_acc[c]] if rotates else [],
                )
                if rotates:
                    item_acc[c] = moved(updated[0], 1, 0)
                elif updated:
                    items[c], item_acc[c] = updated
            terms[c] = group_terms(term)
        users, user_acc = adagrad(users, user_acc, grad_user)
    filled = []
    for c in range(CHUNKS):
        filled = [last_item_step(rows[c], item_factors.shape[0], items[c], item_acc[c], terms[c], filled)]
    return (users, filled[0])


def solution(mesh):
    in_specs = (
        P(None, ("loop", "grp"), None),
        P(("loop", "grp"), None),
        P(("loop", "grp"), None),
        P("loop", None),
        P("loop", None),
    )
    out_specs = (P(("loop", "grp"), None), P("loop", None))
    return jax.shard_map(local, mesh=mesh, in_specs=in_specs, out_specs=out_specs, check_vma=False)
```

```python
import functools

import jax
import jax.numpy as jnp
from jax import lax
from jax.experimental import pallas as pl
from jax.experimental.pallas import tpu as pltpu
from jax.sharding import PartitionSpec as P

SUB = 2
INNER = 2
CHUNKS = 4
FIRST = 2
TILE = 256


shrink = 0.05
learn_rate = 0.2
tiny_eps = 1e-06


def moved(shard, loop_by, grp_by):
    loops, groups = lax.axis_size("loop"), lax.axis_size("grp")
    pairs = [
        (w * groups + g, (w + loop_by) % loops * groups + (g + grp_by) % groups)
        for w in range(loops)
        for g in range(groups)
    ]
    return lax.ppermute(shard, ("loop", "grp"), pairs)


def adagrad(param, accum, grad):
    accum = accum + grad * grad
    return (param - learn_rate * grad * lax.rsqrt(accum + tiny_eps), accum)


def group_terms(term):
    if lax.axis_size("grp") == 2:
        return (term, moved(term, 0, 1))
    return (lax.psum(term, "grp"),)


def item_step(items, accum, terms):
    items = items.astype(jnp.float32)
    grad = sum(term.astype(jnp.float32) for term in terms) + shrink * items
    return adagrad(items, accum.astype(jnp.float32), grad)


def chunk_tile(half, half_t, items, rate):
    item_half = items.astype(jnp.bfloat16)
    predicted = lax.dot_general(
        half, item_half, (((1,), (1,)), ((), ())), preferred_element_type=jnp.float32
    )
    rate = rate.astype(jnp.float32)
    resid = jnp.where(jnp.abs(rate) > 0.25, rate - predicted, 0.0).astype(jnp.bfloat16)
    term = jnp.dot(half_t, resid, preferred_element_type=jnp.float32)
    return (-term).T.astype(jnp.bfloat16), jnp.dot(resid, item_half, preferred_element_type=jnp.float32)


def params(mib=16):
    return pltpu.CompilerParams(vmem_limit_bytes=mib * 2**20)


def cost(users, items, rank):
    return pl.CostEstimate(
        flops=6 * users * items * rank, bytes_accessed=2 * users * items, transcendentals=0
    )


WHOLE = pl.BlockSpec(memory_space=pltpu.VMEM)
AWAY = pl.BlockSpec(memory_space=pltpu.HBM)


def first_kernel(column, rate_hbm, items_hbm, users_hbm, term_out, grad_out, half_out, *scratch):
    users_ref, rate_ref, items_ref, sems = scratch
    load_users = pltpu.make_async_copy(users_hbm, users_ref, sems.at[2, 0])
    load_users.start()
    tiles = range(term_out.shape[0] // TILE)
    loads = []
    for t in tiles:
        at = pl.ds(column + t * TILE, TILE)
        loads.append(
            (
                pltpu.make_async_copy(items_hbm.at[at, :], items_ref.at[t], sems.at[0, t]),
                pltpu.make_async_copy(rate_hbm.at[0, :, at], rate_ref.at[t], sems.at[1, t]),
            )
        )
        for load in loads[-1]:
            load.start()
    load_users.wait()
    grad = shrink * users_ref[...]
    half = users_ref[...].astype(jnp.bfloat16)
    half_t = half.T
    half_out[...] = half
    for t in tiles:
        for load in loads[t]:
            load.wait()
        term, part = chunk_tile(half, half_t, items_ref[t], rate_ref[t])
        term_out[pl.ds(t * TILE, TILE), :] = term
        grad = grad - part
    grad_out[...] = grad


def first_pass(ratings, rows, users, items):
    size, (n_users, rank) = rows.stop - rows.start, users.shape
    return pl.pallas_call(
        functools.partial(first_kernel, rows.start),
        out_shape=[
            jax.ShapeDtypeStruct((size, rank), jnp.bfloat16),
            jax.ShapeDtypeStruct(users.shape, jnp.float32),
            jax.ShapeDtypeStruct(users.shape, jnp.bfloat16),
        ],
        in_specs=[AWAY] * 3,
        out_specs=[WHOLE] * 3,
        scratch_shapes=[
            pltpu.VMEM(users.shape, jnp.float32),
            pltpu.VMEM((size // TILE, n_users, TILE), jnp.bfloat16),
            pltpu.VMEM((size // TILE, TILE, rank), jnp.float32),
            pltpu.SemaphoreType.DMA((3, size // TILE)),
        ],
        compiler_params=params(62),
        cost_estimate=cost(n_users, size, rank),
    )(ratings, items, users)


def chunk_kernel(n_terms, sub_epoch, column, items_at, accum_at, terms_at, rate_ref, half_ref, grad_ref, items_ref, *refs):
    term_refs, refs = refs[:n_terms], refs[n_terms:]
    if n_terms:
        accum_ref, *refs = refs
    term_out, grad_out, *updated = refs
    half = half_ref[...]
    half_t = half.T
    grad = grad_ref[...]
    for start in range(0, term_out.shape[0], TILE):
        at = pl.ds(start, TILE)
        items = items_ref[pl.ds(items_at + start, TILE), :]
        if n_terms:
            accum = accum_ref[pl.ds(accum_at + start, TILE), :]
            items, accum = item_step(items, accum, [ref[pl.ds(terms_at + start, TILE), :] for ref in term_refs])
            updated[0][at, :] = items
            updated[1][at, :] = accum
        term_out[at, :], part = chunk_tile(
            half, half_t, items, rate_ref[sub_epoch, :, pl.ds(column + start, TILE)]
        )
        grad = grad - part
    grad_out[...] = grad


def chunk_pass(ratings, sub_epoch, rows, half, grad, items, accum, terms, terms_at):
    size, rank = rows.stop - rows.start, half.shape[1]
    out_shape = [
        jax.ShapeDtypeStruct((size, rank), jnp.bfloat16),
        jax.ShapeDtypeStruct(grad.shape, jnp.float32),
    ]
    operands = [ratings, half, grad, items[0]]
    if terms:
        out_shape += [jax.ShapeDtypeStruct((size, rank), jnp.float32)] * 2
        operands += [*terms, accum[0]]
    return pl.pallas_call(
        functools.partial(chunk_kernel, len(terms), sub_epoch, rows.start, items[1], accum[1], terms_at),
        out_shape=out_shape,
        in_specs=[WHOLE] * len(operands),
        out_specs=[WHOLE] * len(out_shape),
        compiler_params=params(),
        cost_estimate=cost(half.shape[0], size, rank),
    )(*operands)


def parting_kernel(n_terms, n_behind, items_ref, accum_ref, *refs):
    size = items_ref.shape[0]
    items, accum = item_step(items_ref[...], accum_ref[...], [ref[...] for ref in refs[:n_terms]])
    sent, accum_out = refs[-2:]
    sent[pl.ds(0, size), :] = items.astype(jnp.bfloat16)
    if n_behind:
        sent[pl.ds(size, size), :] = refs[n_terms][...]
    accum_out[...] = accum.astype(jnp.bfloat16)


def parting_step(items, accum, terms, behind, after):
    size, rank = items.shape
    return pl.pallas_call(
        functools.partial(parting_kernel, len(terms), len(behind)),
        out_shape=[
            jax.ShapeDtypeStruct((size * (1 + len(behind)), rank), jnp.bfloat16),
            jax.ShapeDtypeStruct((size, rank), jnp.bfloat16),
        ],
        in_specs=[WHOLE] * (2 + len(terms) + len(behind)) + [pl.BlockSpec(memory_space=pl.ANY)] * len(after),
        out_specs=[WHOLE] * 2,
        compiler_params=params(),
        cost_estimate=cost(1, size, rank),
    )(items, accum, *terms, *behind, *after)


def last_kernel(n_terms, row, items_ref, accum_ref, *refs):
    out_hbm, out_ref, sems = refs[-3:]
    stores = []
    for t in range(items_ref.shape[0] // TILE):
        at = pl.ds(t * TILE, TILE)
        out_ref[at, :], _ = item_step(items_ref[at, :], accum_ref[at, :], [ref[at, :] for ref in refs[:n_terms]])
        stores.append(
            pltpu.make_async_copy(out_ref.at[at, :], out_hbm.at[pl.ds(row + t * TILE, TILE), :], sems.at[t])
        )
        stores[-1].start()
    for store in stores:
        store.wait()


def last_item_step(rows, n_items, items, accum, terms, filled):
    size, rank = items.shape
    return pl.pallas_call(
        functools.partial(last_kernel, len(terms), rows.start),
        out_shape=jax.ShapeDtypeStruct((n_items, rank), jnp.float32),
        in_specs=[WHOLE] * (2 + len(terms)) + [AWAY] * len(filled),
        out_specs=AWAY,
        scratch_shapes=[
            pltpu.VMEM((size, rank), jnp.float32),
            pltpu.SemaphoreType.DMA((size // TILE,)),
        ],
        input_output_aliases={2 + len(terms): 0} if filled else {},
        compiler_params=params(),
        cost_estimate=cost(1, size, rank),
    )(items, accum, *terms, *filled)


def local(ratings, user_factors, user_accum, item_factors, item_accum):
    users = user_factors
    user_acc = user_accum
    size = item_factors.shape[0] // CHUNKS
    rows = [slice(c * size, (c + 1) * size) for c in range(CHUNKS)]
    items = [(item_factors, r.start) for r in rows]
    item_acc = [(item_accum, r.start) for r in rows]
    terms = [()] * CHUNKS
    behind = []

    def part(c, after):
        nonlocal behind
        sent, accum = parting_step(items[c][0], item_acc[c][0], terms[c], behind, after)
        items[c] = (moved(sent, 1, 0), 0)
        if c > 0:
            item_acc[c - 1] = (items[c][0], size)
        behind, terms[c] = [accum], ()

    for step in range(SUB * INNER):
        sub_epoch = step // INNER
        rotates = step > 0 and step % INNER == 0
        if rotates:
            behind = []
            for c in range(CHUNKS - 1):
                part(c, [])
        if step > 0:
            user_half = users.astype(jnp.bfloat16)
            grad_user = shrink * users
        for c in range(CHUNKS):
            if rotates and c == 1:
                part(CHUNKS - 1, [term])
                item_acc[CHUNKS - 1] = (moved(behind[0], 1, 0), 0)
            if step == 0:
                if c % FIRST:
                    terms[c] = terms[c - 1]
                    continue
                both = slice(rows[c].start, rows[c + FIRST - 1].stop)
                if c == 0:
                    term, grad_user, user_half = first_pass(ratings, both, users, item_factors)
                else:
                    term, grad_user = chunk_pass(ratings, 0, both, user_half, grad_user, items[c], item_acc[c], (), 0)
            else:
                term, grad_user, *updated = chunk_pass(
                    ratings, sub_epoch, rows[c], user_half, grad_user, items[c], item_acc[c], terms[c],
                    c % FIRST * size if step == 1 else 0,
                )
                if updated:
                    items[c], item_acc[c] = ((array, 0) for array in updated)
            terms[c] = group_terms(term)
        users, user_acc = adagrad(users, user_acc, grad_user)
    filled = []
    for c in range(CHUNKS):
        filled = [last_item_step(rows[c], item_factors.shape[0], items[c][0], item_acc[c][0], terms[c], filled)]
    return (users, filled[0])


def solution(mesh):
    in_specs = (
        P(None, ("loop", "grp"), None),
        P(("loop", "grp"), None),
        P(("loop", "grp"), None),
        P("loop", None),
        P("loop", None),
    )
    out_specs = (P(("loop", "grp"), None), P("loop", None))
    return jax.shard_map(local, mesh=mesh, in_specs=in_specs, out_specs=out_specs, check_vma=False)
```

```python
import functools

import jax
import jax.numpy as jnp
from jax import lax
from jax.experimental import pallas as pl
from jax.experimental.pallas import tpu as pltpu
from jax.sharding import PartitionSpec as P

SUB = 2
INNER = 2
CHUNKS = 4
FIRST = 2
TILE = 256


shrink = 0.05
learn_rate = 0.2
tiny_eps = 1e-06


def moved(shard, loop_by, grp_by):
    loops, groups = lax.axis_size("loop"), lax.axis_size("grp")
    pairs = [
        (w * groups + g, (w + loop_by) % loops * groups + (g + grp_by) % groups)
        for w in range(loops)
        for g in range(groups)
    ]
    return lax.ppermute(shard, ("loop", "grp"), pairs)


def adagrad(param, accum, grad):
    accum = accum + grad * grad
    return (param - learn_rate * grad * lax.rsqrt(accum + tiny_eps), accum)


def group_terms(term):
    if lax.axis_size("grp") == 2:
        return (term, moved(term, 0, 1))
    return (lax.psum(term, "grp"),)


def item_step(items, accum, terms):
    items = items.astype(jnp.float32)
    grad = sum(term.astype(jnp.float32) for term in terms) + shrink * items
    return adagrad(items, accum.astype(jnp.float32), grad)


def chunk_tile(half, half_t, items, rate):
    item_half = items.astype(jnp.bfloat16)
    predicted = lax.dot_general(
        half, item_half, (((1,), (1,)), ((), ())), preferred_element_type=jnp.float32
    )
    rate = rate.astype(jnp.float32)
    resid = jnp.where(jnp.abs(rate) > 0.25, rate - predicted, 0.0).astype(jnp.bfloat16)
    term = jnp.dot(half_t, resid, preferred_element_type=jnp.float32)
    return (-term).T.astype(jnp.bfloat16), jnp.dot(resid, item_half, preferred_element_type=jnp.float32)


def params(mib=16):
    return pltpu.CompilerParams(vmem_limit_bytes=mib * 2**20)


def cost(users, items, rank):
    return pl.CostEstimate(
        flops=6 * users * items * rank, bytes_accessed=2 * users * items, transcendentals=0
    )


WHOLE = pl.BlockSpec(memory_space=pltpu.VMEM)
AWAY = pl.BlockSpec(memory_space=pltpu.HBM)


def first_kernel(column, rate_hbm, items_hbm, users_hbm, term_out, grad_out, half_out, *scratch):
    users_ref, rate_ref, items_ref, sems = scratch
    load_users = pltpu.make_async_copy(users_hbm, users_ref, sems.at[2, 0])
    load_users.start()
    tiles = range(term_out.shape[0] // TILE)
    loads = []
    for t in tiles:
        at = pl.ds(column + t * TILE, TILE)
        loads.append(
            (
                pltpu.make_async_copy(items_hbm.at[at, :], items_ref.at[t], sems.at[0, t]),
                pltpu.make_async_copy(rate_hbm.at[0, :, at], rate_ref.at[t], sems.at[1, t]),
            )
        )
        for load in loads[-1]:
            load.start()
    load_users.wait()
    grad = shrink * users_ref[...]
    half = users_ref[...].astype(jnp.bfloat16)
    half_t = half.T
    half_out[...] = half
    for t in tiles:
        for load in loads[t]:
            load.wait()
        term, part = chunk_tile(half, half_t, items_ref[t], rate_ref[t])
        term_out[pl.ds(t * TILE, TILE), :] = term
        grad = grad - part
    grad_out[...] = grad


def first_pass(ratings, rows, users, items):
    size, (n_users, rank) = rows.stop - rows.start, users.shape
    return pl.pallas_call(
        functools.partial(first_kernel, rows.start),
        out_shape=[
            jax.ShapeDtypeStruct((size, rank), jnp.bfloat16),
            jax.ShapeDtypeStruct(users.shape, jnp.float32),
            jax.ShapeDtypeStruct(users.shape, jnp.bfloat16),
        ],
        in_specs=[AWAY] * 3,
        out_specs=[WHOLE] * 3,
        scratch_shapes=[
            pltpu.VMEM(users.shape, jnp.float32),
            pltpu.VMEM((size // TILE, n_users, TILE), jnp.bfloat16),
            pltpu.VMEM((size // TILE, TILE, rank), jnp.float32),
            pltpu.SemaphoreType.DMA((3, size // TILE)),
        ],
        compiler_params=params(62),
        cost_estimate=cost(n_users, size, rank),
    )(ratings, items, users)


def chunk_kernel(n_terms, n_after, sub_epoch, column, items_at, accum_at, terms_at, rate_ref, half_ref, grad_ref, items_ref, *refs):
    term_refs, refs = refs[:n_terms], refs[n_terms:]
    if n_terms:
        accum_ref, *refs = refs
    term_out, grad_out, *updated = refs[n_after:]
    half = half_ref[...]
    half_t = half.T
    grad = grad_ref[...]
    for start in range(0, term_out.shape[0], TILE):
        at = pl.ds(start, TILE)
        items = items_ref[pl.ds(items_at + start, TILE), :]
        if n_terms:
            accum = accum_ref[pl.ds(accum_at + start, TILE), :]
            items, accum = item_step(items, accum, [ref[pl.ds(terms_at + start, TILE), :] for ref in term_refs])
            updated[0][at, :] = items
            updated[1][at, :] = accum
        term_out[at, :], part = chunk_tile(
            half, half_t, items, rate_ref[sub_epoch, :, pl.ds(column + start, TILE)]
        )
        grad = grad - part
    grad_out[...] = grad


def chunk_pass(ratings, sub_epoch, rows, half, grad, items, accum, terms, terms_at, after=()):
    size, rank = rows.stop - rows.start, half.shape[1]
    out_shape = [
        jax.ShapeDtypeStruct((size, rank), jnp.bfloat16),
        jax.ShapeDtypeStruct(grad.shape, jnp.float32),
    ]
    operands = [ratings, half, grad, items[0]]
    if terms:
        out_shape += [jax.ShapeDtypeStruct((size, rank), jnp.float32)] * 2
        operands += [*terms, accum[0]]
    return pl.pallas_call(
        functools.partial(chunk_kernel, len(terms), len(after), sub_epoch, rows.start, items[1], accum[1], terms_at),
        out_shape=out_shape,
        in_specs=[WHOLE] * len(operands) + [pl.BlockSpec(memory_space=pl.ANY)] * len(after),
        out_specs=[WHOLE] * len(out_shape),
        compiler_params=params(),
        cost_estimate=cost(half.shape[0], size, rank),
    )(*operands, *after)


def parting_kernel(n_terms, n_behind, items_ref, accum_ref, *refs):
    size = items_ref.shape[0]
    items, accum = item_step(items_ref[...], accum_ref[...], [ref[...] for ref in refs[:n_terms]])
    sent, accum_out = refs[-2:]
    sent[pl.ds(0, size), :] = items.astype(jnp.bfloat16)
    if n_behind:
        sent[pl.ds(size, size), :] = refs[n_terms][...]
    accum_out[...] = accum.astype(jnp.bfloat16)


def parting_step(items, accum, terms, behind, after):
    size, rank = items.shape
    return pl.pallas_call(
        functools.partial(parting_kernel, len(terms), len(behind)),
        out_shape=[
            jax.ShapeDtypeStruct((size * (1 + len(behind)), rank), jnp.bfloat16),
            jax.ShapeDtypeStruct((size, rank), jnp.bfloat16),
        ],
        in_specs=[WHOLE] * (2 + len(terms) + len(behind)) + [pl.BlockSpec(memory_space=pl.ANY)] * len(after),
        out_specs=[WHOLE] * 2,
        compiler_params=params(),
        cost_estimate=cost(1, size, rank),
    )(items, accum, *terms, *behind, *after)


def last_kernel(n_terms, row, items_ref, accum_ref, *refs):
    out_hbm, out_ref, sems = refs[-3:]
    stores = []
    for t in range(items_ref.shape[0] // TILE):
        at = pl.ds(t * TILE, TILE)
        out_ref[at, :], _ = item_step(items_ref[at, :], accum_ref[at, :], [ref[at, :] for ref in refs[:n_terms]])
        stores.append(
            pltpu.make_async_copy(out_ref.at[at, :], out_hbm.at[pl.ds(row + t * TILE, TILE), :], sems.at[t])
        )
        stores[-1].start()
    for store in stores:
        store.wait()


def last_item_step(rows, n_items, items, accum, terms, filled):
    size, rank = items.shape
    return pl.pallas_call(
        functools.partial(last_kernel, len(terms), rows.start),
        out_shape=jax.ShapeDtypeStruct((n_items, rank), jnp.float32),
        in_specs=[WHOLE] * (2 + len(terms)) + [AWAY] * len(filled),
        out_specs=AWAY,
        scratch_shapes=[
            pltpu.VMEM((size, rank), jnp.float32),
            pltpu.SemaphoreType.DMA((size // TILE,)),
        ],
        input_output_aliases={2 + len(terms): 0} if filled else {},
        compiler_params=params(),
        cost_estimate=cost(1, size, rank),
    )(items, accum, *terms, *filled)


def local(ratings, user_factors, user_accum, item_factors, item_accum):
    users = user_factors
    user_acc = user_accum
    size = item_factors.shape[0] // CHUNKS
    rows = [slice(c * size, (c + 1) * size) for c in range(CHUNKS)]
    items = [(item_factors, r.start) for r in rows]
    item_acc = [(item_accum, r.start) for r in rows]
    terms = [()] * CHUNKS
    behind = []

    def part(c, after):
        nonlocal behind
        sent, accum = parting_step(items[c][0], item_acc[c][0], terms[c], behind, after)
        items[c] = (moved(sent, 1, 0), 0)
        if c > 0:
            item_acc[c - 1] = (items[c][0], size)
        behind, terms[c] = [accum], ()
        return [sent]

    for step in range(SUB * INNER):
        sub_epoch = step // INNER
        rotates = step > 0 and step % INNER == 0
        if rotates:
            for c in range(1, CHUNKS - 1):
                part(c, [term])
        if step > 0:
            user_half = users.astype(jnp.bfloat16)
            grad_user = shrink * users
        for c in range(CHUNKS):
            if rotates and c == 1:
                part(CHUNKS - 1, [term])
                item_acc[CHUNKS - 1] = (moved(behind[0], 1, 0), 0)
            after = []
            if c == CHUNKS - 1 and step % INNER == INNER - 1 and sub_epoch < SUB - 1:
                behind = []
                after = part(0, [])
            if step == 0:
                if c % FIRST:
                    terms[c] = terms[c - 1]
                    continue
                both = slice(rows[c].start, rows[c + FIRST - 1].stop)
                if c == 0:
                    term, grad_user, user_half = first_pass(ratings, both, users, item_factors)
                else:
                    term, grad_user = chunk_pass(ratings, 0, both, user_half, grad_user, items[c], item_acc[c], (), 0)
            else:
                term, grad_user, *updated = chunk_pass(
                    ratings, sub_epoch, rows[c], user_half, grad_user, items[c], item_acc[c], terms[c],
                    c % FIRST * size if step == 1 else 0, after,
                )
                if updated:
                    items[c], item_acc[c] = ((array, 0) for array in updated)
            terms[c] = group_terms(term)
        users, user_acc = adagrad(users, user_acc, grad_user)
    filled = []
    for c in range(CHUNKS):
        filled = [last_item_step(rows[c], item_factors.shape[0], items[c][0], item_acc[c][0], terms[c], filled)]
    return (users, filled[0])


def solution(mesh):
    in_specs = (
        P(None, ("loop", "grp"), None),
        P(("loop", "grp"), None),
        P(("loop", "grp"), None),
        P("loop", None),
        P("loop", None),
    )
    out_specs = (P(("loop", "grp"), None), P("loop", None))
    return jax.shard_map(local, mesh=mesh, in_specs=in_specs, out_specs=out_specs, check_vma=False)
```

```python
import functools

import jax
import jax.numpy as jnp
from jax import lax
from jax.experimental import pallas as pl
from jax.experimental.pallas import tpu as pltpu
from jax.sharding import PartitionSpec as P

SUB = 2
INNER = 2
CHUNKS = 4
FIRST = 2
LAST = 2
TILE = 256


shrink = 0.05
learn_rate = 0.2
tiny_eps = 1e-06


def moved(shard, loop_by, grp_by):
    loops, groups = lax.axis_size("loop"), lax.axis_size("grp")
    pairs = [
        (w * groups + g, (w + loop_by) % loops * groups + (g + grp_by) % groups)
        for w in range(loops)
        for g in range(groups)
    ]
    return lax.ppermute(shard, ("loop", "grp"), pairs)


def adagrad(param, accum, grad):
    accum = accum + grad * grad
    return (param - learn_rate * grad * lax.rsqrt(accum + tiny_eps), accum)


def group_terms(term):
    if lax.axis_size("grp") == 2:
        return (term, moved(term, 0, 1))
    return (lax.psum(term, "grp"),)


def item_step(items, accum, terms):
    items = items.astype(jnp.float32)
    grad = sum(term.astype(jnp.float32) for term in terms) + shrink * items
    return adagrad(items, accum.astype(jnp.float32), grad)


def chunk_tile(half, half_t, items, rate):
    item_half = items.astype(jnp.bfloat16)
    predicted = lax.dot_general(
        half, item_half, (((1,), (1,)), ((), ())), preferred_element_type=jnp.float32
    )
    rate = rate.astype(jnp.float32)
    resid = jnp.where(jnp.abs(rate) > 0.25, rate - predicted, 0.0).astype(jnp.bfloat16)
    term = jnp.dot(half_t, resid, preferred_element_type=jnp.float32)
    return (-term).T.astype(jnp.bfloat16), jnp.dot(resid, item_half, preferred_element_type=jnp.float32)


def params(mib=16):
    return pltpu.CompilerParams(vmem_limit_bytes=mib * 2**20)


def cost(users, items, rank):
    return pl.CostEstimate(
        flops=6 * users * items * rank, bytes_accessed=2 * users * items, transcendentals=0
    )


WHOLE = pl.BlockSpec(memory_space=pltpu.VMEM)
AWAY = pl.BlockSpec(memory_space=pltpu.HBM)


def first_kernel(column, rate_hbm, items_hbm, users_hbm, term_out, grad_out, half_out, *scratch):
    users_ref, rate_ref, items_ref, sems = scratch
    load_users = pltpu.make_async_copy(users_hbm, users_ref, sems.at[2, 0])
    load_users.start()
    tiles = range(term_out.shape[0] // TILE)
    loads = []
    for t in tiles:
        at = pl.ds(column + t * TILE, TILE)
        loads.append(
            (
                pltpu.make_async_copy(items_hbm.at[at, :], items_ref.at[t], sems.at[0, t]),
                pltpu.make_async_copy(rate_hbm.at[0, :, at], rate_ref.at[t], sems.at[1, t]),
            )
        )
        for load in loads[-1]:
            load.start()
    load_users.wait()
    grad = shrink * users_ref[...]
    half = users_ref[...].astype(jnp.bfloat16)
    half_t = half.T
    half_out[...] = half
    for t in tiles:
        for load in loads[t]:
            load.wait()
        term, part = chunk_tile(half, half_t, items_ref[t], rate_ref[t])
        term_out[pl.ds(t * TILE, TILE), :] = term
        grad = grad - part
    grad_out[...] = grad


def first_pass(ratings, rows, users, items):
    size, (n_users, rank) = rows.stop - rows.start, users.shape
    return pl.pallas_call(
        functools.partial(first_kernel, rows.start),
        out_shape=[
            jax.ShapeDtypeStruct((size, rank), jnp.bfloat16),
            jax.ShapeDtypeStruct(users.shape, jnp.float32),
            jax.ShapeDtypeStruct(users.shape, jnp.bfloat16),
        ],
        in_specs=[AWAY] * 3,
        out_specs=[WHOLE] * 3,
        scratch_shapes=[
            pltpu.VMEM(users.shape, jnp.float32),
            pltpu.VMEM((size // TILE, n_users, TILE), jnp.bfloat16),
            pltpu.VMEM((size // TILE, TILE, rank), jnp.float32),
            pltpu.SemaphoreType.DMA((3, size // TILE)),
        ],
        compiler_params=params(62),
        cost_estimate=cost(n_users, size, rank),
    )(ratings, items, users)


def chunk_kernel(sub_epoch, column, size, places, rate_ref, half_ref, grad_ref, *refs):
    half = half_ref[...]
    half_t = half.T
    grad = grad_ref[...]
    term_out, grad_out, *updated = refs[-4:] if places[0][0] else refs[-2:]
    for piece, (n_terms, items_at, accum_at, terms_at) in enumerate(places):
        items_ref, *refs = refs
        if n_terms:
            accum_ref, *refs = refs
            term_refs, refs = refs[:n_terms], refs[n_terms:]
        for start in range(0, size, TILE):
            at = pl.ds(piece * size + start, TILE)
            items = items_ref[pl.ds(items_at + start, TILE), :]
            if n_terms:
                accum = accum_ref[pl.ds(accum_at + start, TILE), :]
                terms = [ref[pl.ds(terms_at + start, TILE), :] for ref in term_refs]
                items, accum = item_step(items, accum, terms)
                updated[0][at, :] = items
                updated[1][at, :] = accum
            rate = rate_ref[sub_epoch, :, pl.ds(column + piece * size + start, TILE)]
            term_out[at, :], part = chunk_tile(half, half_t, items, rate)
            grad = grad - part
    grad_out[...] = grad


def chunk_pass(ratings, sub_epoch, rows, half, grad, pieces, after=()):
    total, rank = rows.stop - rows.start, half.shape[1]
    out_shape = [
        jax.ShapeDtypeStruct((total, rank), jnp.bfloat16),
        jax.ShapeDtypeStruct(grad.shape, jnp.float32),
    ]
    operands, places = [ratings, half, grad], []
    for items, accum, terms, terms_at in pieces:
        operands += [items[0], accum[0], *terms] if terms else [items[0]]
        places.append((len(terms), items[1], accum[1], terms_at))
    if places[0][0]:
        out_shape += [jax.ShapeDtypeStruct((total, rank), jnp.float32)] * 2
    return pl.pallas_call(
        functools.partial(chunk_kernel, sub_epoch, rows.start, total // len(pieces), places),
        out_shape=out_shape,
        in_specs=[WHOLE] * len(operands) + [pl.BlockSpec(memory_space=pl.ANY)] * len(after),
        out_specs=[WHOLE] * len(out_shape),
        compiler_params=params(),
        cost_estimate=cost(half.shape[0], total, rank),
    )(*operands, *after)


def parting_kernel(n_terms, n_behind, items_ref, accum_ref, *refs):
    size = items_ref.shape[0]
    items, accum = item_step(items_ref[...], accum_ref[...], [ref[...] for ref in refs[:n_terms]])
    sent, accum_out = refs[-2:]
    sent[pl.ds(0, size), :] = items.astype(jnp.bfloat16)
    if n_behind:
        sent[pl.ds(size, size), :] = refs[n_terms][...]
    accum_out[...] = accum.astype(jnp.bfloat16)


def parting_step(items, accum, terms, behind, after):
    size, rank = items.shape
    return pl.pallas_call(
        functools.partial(parting_kernel, len(terms), len(behind)),
        out_shape=[
            jax.ShapeDtypeStruct((size * (1 + len(behind)), rank), jnp.bfloat16),
            jax.ShapeDtypeStruct((size, rank), jnp.bfloat16),
        ],
        in_specs=[WHOLE] * (2 + len(terms) + len(behind)) + [pl.BlockSpec(memory_space=pl.ANY)] * len(after),
        out_specs=[WHOLE] * 2,
        compiler_params=params(),
        cost_estimate=cost(1, size, rank),
    )(items, accum, *terms, *behind, *after)


def last_kernel(n_terms, row, items_ref, accum_ref, *refs):
    out_hbm, out_ref, sems = refs[-3:]
    stores = []
    for t in range(items_ref.shape[0] // TILE):
        at = pl.ds(t * TILE, TILE)
        out_ref[at, :], _ = item_step(items_ref[at, :], accum_ref[at, :], [ref[at, :] for ref in refs[:n_terms]])
        stores.append(
            pltpu.make_async_copy(out_ref.at[at, :], out_hbm.at[pl.ds(row + t * TILE, TILE), :], sems.at[t])
        )
        stores[-1].start()
    for store in stores:
        store.wait()


def last_item_step(rows, n_items, items, accum, terms, filled):
    size, rank = items.shape
    return pl.pallas_call(
        functools.partial(last_kernel, len(terms), rows.start),
        out_shape=jax.ShapeDtypeStruct((n_items, rank), jnp.float32),
        in_specs=[WHOLE] * (2 + len(terms)) + [AWAY] * len(filled),
        out_specs=AWAY,
        scratch_shapes=[
            pltpu.VMEM((size, rank), jnp.float32),
            pltpu.SemaphoreType.DMA((size // TILE,)),
        ],
        input_output_aliases={2 + len(terms): 0} if filled else {},
        compiler_params=params(),
        cost_estimate=cost(1, size, rank),
    )(items, accum, *terms, *filled)


def local(ratings, user_factors, user_accum, item_factors, item_accum):
    users = user_factors
    user_acc = user_accum
    size = item_factors.shape[0] // CHUNKS
    rows = [slice(c * size, (c + 1) * size) for c in range(CHUNKS)]
    items = [(item_factors, r.start) for r in rows]
    item_acc = [(item_accum, r.start) for r in rows]
    terms = [()] * CHUNKS
    behind = []

    def part(c, after):
        nonlocal behind
        sent, accum = parting_step(items[c][0], item_acc[c][0], terms[c], behind, after)
        items[c] = (moved(sent, 1, 0), 0)
        if c > 0:
            item_acc[c - 1] = (items[c][0], size)
        behind, terms[c] = [accum], ()
        return [sent]

    for step in range(SUB * INNER):
        sub_epoch = step // INNER
        rotates = step > 0 and step % INNER == 0
        if rotates:
            for c in range(1, CHUNKS - 1):
                part(c, [term])
        if step > 0:
            user_half = users.astype(jnp.bfloat16)
            grad_user = shrink * users
        for c in range(CHUNKS):
            if rotates and c == 1:
                part(CHUNKS - 1, [term])
                item_acc[CHUNKS - 1] = (moved(behind[0], 1, 0), 0)
            after = []
            if c == CHUNKS - 1 and step % INNER == INNER - 1 and sub_epoch < SUB - 1:
                behind = []
                after = part(0, [])
            if step == 0:
                if c % FIRST:
                    terms[c] = terms[c - 1]
                    continue
                both = slice(rows[c].start, rows[c + FIRST - 1].stop)
                if c == 0:
                    term, grad_user, user_half = first_pass(ratings, both, users, item_factors)
                else:
                    piece = (items[c], item_acc[c], (), 0)
                    term, grad_user = chunk_pass(ratings, 0, both, user_half, grad_user, [piece])
            else:
                taken = [c]
                if step == SUB * INNER - 1:
                    if c % LAST:
                        continue
                    taken = range(c, c + LAST)
                at = [d % FIRST * size if step == 1 else 0 for d in taken]
                term, grad_user, *updated = chunk_pass(
                    ratings, sub_epoch, slice(rows[c].start, rows[taken[-1]].stop), user_half, grad_user,
                    [(items[d], item_acc[d], terms[d], row) for d, row in zip(taken, at)], after,
                )
                if updated:
                    items[c], item_acc[c] = ((array, 0) for array in updated)
            terms[c] = group_terms(term)
        users, user_acc = adagrad(users, user_acc, grad_user)
    filled = []
    for c in range(0, CHUNKS, LAST):
        filled = [last_item_step(rows[c], item_factors.shape[0], items[c][0], item_acc[c][0], terms[c], filled)]
    return (users, filled[0])


def solution(mesh):
    in_specs = (
        P(None, ("loop", "grp"), None),
        P(("loop", "grp"), None),
        P(("loop", "grp"), None),
        P("loop", None),
        P("loop", None),
    )
    out_specs = (P(("loop", "grp"), None), P("loop", None))
    return jax.shard_map(local, mesh=mesh, in_specs=in_specs, out_specs=out_specs, check_vma=False)
```

```python
import functools

import jax
import jax.numpy as jnp
from jax import lax
from jax.experimental import pallas as pl
from jax.experimental.pallas import tpu as pltpu
from jax.sharding import PartitionSpec as P

SUB = 2
INNER = 2
CHUNKS = 4
FIRST = 2
LAST = 2
TILE = 256


shrink = 0.05
learn_rate = 0.2
tiny_eps = 1e-06


def moved(shard, loop_by, grp_by):
    loops, groups = lax.axis_size("loop"), lax.axis_size("grp")
    pairs = [
        (w * groups + g, (w + loop_by) % loops * groups + (g + grp_by) % groups)
        for w in range(loops)
        for g in range(groups)
    ]
    return lax.ppermute(shard, ("loop", "grp"), pairs)


def adagrad(param, accum, grad):
    accum = accum + grad * grad
    return (param - learn_rate * grad * lax.rsqrt(accum + tiny_eps), accum)


def group_terms(term):
    if lax.axis_size("grp") == 2:
        return (term, moved(term, 0, 1))
    return (lax.psum(term, "grp"),)


def item_step(items, accum, terms):
    items = items.astype(jnp.float32)
    grad = sum(term.astype(jnp.float32) for term in terms) + shrink * items
    return adagrad(items, accum.astype(jnp.float32), grad)


def chunk_tile(half, half_t, items, rate):
    item_half = items.astype(jnp.bfloat16)
    predicted = lax.dot_general(
        half, item_half, (((1,), (1,)), ((), ())), preferred_element_type=jnp.float32
    )
    rate = rate.astype(jnp.float32)
    resid = jnp.where(jnp.abs(rate) > 0.25, rate - predicted, 0.0).astype(jnp.bfloat16)
    term = jnp.dot(half_t, resid, preferred_element_type=jnp.float32)
    return (-term).T.astype(jnp.bfloat16), jnp.dot(resid, item_half, preferred_element_type=jnp.float32)


def params(mib=16):
    return pltpu.CompilerParams(vmem_limit_bytes=mib * 2**20)


def cost(users, items, rank):
    return pl.CostEstimate(
        flops=6 * users * items * rank, bytes_accessed=2 * users * items, transcendentals=0
    )


WHOLE = pl.BlockSpec(memory_space=pltpu.VMEM)
AWAY = pl.BlockSpec(memory_space=pltpu.HBM)


def first_kernel(column, rate_hbm, items_hbm, users_hbm, term_out, grad_out, half_out, *scratch):
    users_ref, rate_ref, items_ref, sems = scratch
    load_users = pltpu.make_async_copy(users_hbm, users_ref, sems.at[2, 0])
    load_users.start()
    tiles = range(term_out.shape[0] // TILE)
    loads = []
    for t in tiles:
        at = pl.ds(column + t * TILE, TILE)
        loads.append(
            (
                pltpu.make_async_copy(items_hbm.at[at, :], items_ref.at[t], sems.at[0, t]),
                pltpu.make_async_copy(rate_hbm.at[0, :, at], rate_ref.at[t], sems.at[1, t]),
            )
        )
        for load in loads[-1]:
            load.start()
    load_users.wait()
    grad = shrink * users_ref[...]
    half = users_ref[...].astype(jnp.bfloat16)
    half_t = half.T
    half_out[...] = half
    for t in tiles:
        for load in loads[t]:
            load.wait()
        term, part = chunk_tile(half, half_t, items_ref[t], rate_ref[t])
        term_out[pl.ds(t * TILE, TILE), :] = term
        grad = grad - part
    grad_out[...] = grad


def first_pass(ratings, rows, users, items):
    size, (n_users, rank) = rows.stop - rows.start, users.shape
    return pl.pallas_call(
        functools.partial(first_kernel, rows.start),
        out_shape=[
            jax.ShapeDtypeStruct((size, rank), jnp.bfloat16),
            jax.ShapeDtypeStruct(users.shape, jnp.float32),
            jax.ShapeDtypeStruct(users.shape, jnp.bfloat16),
        ],
        in_specs=[AWAY] * 3,
        out_specs=[WHOLE] * 3,
        scratch_shapes=[
            pltpu.VMEM(users.shape, jnp.float32),
            pltpu.VMEM((size // TILE, n_users, TILE), jnp.bfloat16),
            pltpu.VMEM((size // TILE, TILE, rank), jnp.float32),
            pltpu.SemaphoreType.DMA((3, size // TILE)),
        ],
        compiler_params=params(62),
        cost_estimate=cost(n_users, size, rank),
    )(ratings, items, users)


def chunk_kernel(sub_epoch, column, size, places, rate_ref, half_ref, grad_ref, *refs):
    half = half_ref[...]
    half_t = half.T
    grad = grad_ref[...]
    term_out, grad_out, *updated = refs[-4:] if places[0][0] else refs[-2:]
    for piece, (n_terms, items_at, accum_at, terms_at) in enumerate(places):
        items_ref, *refs = refs
        if n_terms:
            accum_ref, *refs = refs
            term_refs, refs = refs[:n_terms], refs[n_terms:]
        for start in range(0, size, TILE):
            at = pl.ds(piece * size + start, TILE)
            items = items_ref[pl.ds(items_at + start, TILE), :]
            if n_terms:
                accum = accum_ref[pl.ds(accum_at + start, TILE), :]
                terms = [ref[pl.ds(terms_at + start, TILE), :] for ref in term_refs]
                items, accum = item_step(items, accum, terms)
                updated[0][at, :] = items
                updated[1][at, :] = accum
            rate = rate_ref[sub_epoch, :, pl.ds(column + piece * size + start, TILE)]
            term_out[at, :], part = chunk_tile(half, half_t, items, rate)
            grad = grad - part
    grad_out[...] = grad


def chunk_pass(ratings, sub_epoch, rows, half, grad, pieces, after=()):
    total, rank = rows.stop - rows.start, half.shape[1]
    out_shape = [
        jax.ShapeDtypeStruct((total, rank), jnp.bfloat16),
        jax.ShapeDtypeStruct(grad.shape, jnp.float32),
    ]
    operands, places = [ratings, half, grad], []
    for items, accum, terms, terms_at in pieces:
        operands += [items[0], accum[0], *terms] if terms else [items[0]]
        places.append((len(terms), items[1], accum[1], terms_at))
    if places[0][0]:
        out_shape += [jax.ShapeDtypeStruct((total, rank), jnp.float32)] * 2
    return pl.pallas_call(
        functools.partial(chunk_kernel, sub_epoch, rows.start, total // len(pieces), places),
        out_shape=out_shape,
        in_specs=[WHOLE] * len(operands) + [pl.BlockSpec(memory_space=pl.ANY)] * len(after),
        out_specs=[WHOLE] * len(out_shape),
        compiler_params=params(),
        cost_estimate=cost(half.shape[0], total, rank),
    )(*operands, *after)


def parting_kernel(n_terms, n_held, items_ref, accum_ref, *refs):
    size = items_ref.shape[0]
    term_refs, held = refs[:n_terms], refs[n_terms : n_terms + n_held]
    items, accum = item_step(items_ref[...], accum_ref[...], [ref[...] for ref in term_refs])
    accum = accum.astype(jnp.bfloat16)
    if not n_held:
        items_out, accum_out = refs[-2:]
        accum_out[...] = accum
    else:
        items_out, *accum_outs = refs[-1 - CHUNKS // LAST :]
        for c, part in enumerate([ref[...] for ref in held] + [accum]):
            accum_outs[c // LAST][pl.ds(c % LAST * size, size), :] = part
    items_out[...] = items.astype(jnp.bfloat16)


def parting_step(items, accum, terms, held, after):
    size, rank = items.shape
    accums = [(LAST * size, rank)] * (CHUNKS // LAST) if held else [(size, rank)]
    return pl.pallas_call(
        functools.partial(parting_kernel, len(terms), len(held)),
        out_shape=[jax.ShapeDtypeStruct(shape, jnp.bfloat16) for shape in [(size, rank), *accums]],
        in_specs=[WHOLE] * (2 + len(terms) + len(held)) + [pl.BlockSpec(memory_space=pl.ANY)] * len(after),
        out_specs=[WHOLE] * (1 + len(accums)),
        compiler_params=params(),
        cost_estimate=cost(1, size, rank),
    )(items, accum, *terms, *held, *after)


def last_kernel(n_terms, row, items_ref, accum_ref, *refs):
    out_hbm, out_ref, sems = refs[-3:]
    stores = []
    for t in range(items_ref.shape[0] // TILE):
        at = pl.ds(t * TILE, TILE)
        out_ref[at, :], _ = item_step(items_ref[at, :], accum_ref[at, :], [ref[at, :] for ref in refs[:n_terms]])
        stores.append(
            pltpu.make_async_copy(out_ref.at[at, :], out_hbm.at[pl.ds(row + t * TILE, TILE), :], sems.at[t])
        )
        stores[-1].start()
    for store in stores:
        store.wait()


def last_item_step(rows, n_items, items, accum, terms, filled):
    size, rank = items.shape
    return pl.pallas_call(
        functools.partial(last_kernel, len(terms), rows.start),
        out_shape=jax.ShapeDtypeStruct((n_items, rank), jnp.float32),
        in_specs=[WHOLE] * (2 + len(terms)) + [AWAY] * len(filled),
        out_specs=AWAY,
        scratch_shapes=[
            pltpu.VMEM((size, rank), jnp.float32),
            pltpu.SemaphoreType.DMA((size // TILE,)),
        ],
        input_output_aliases={2 + len(terms): 0} if filled else {},
        compiler_params=params(),
        cost_estimate=cost(1, size, rank),
    )(items, accum, *terms, *filled)


def local(ratings, user_factors, user_accum, item_factors, item_accum):
    users = user_factors
    user_acc = user_accum
    size = item_factors.shape[0] // CHUNKS
    rows = [slice(c * size, (c + 1) * size) for c in range(CHUNKS)]
    items = [(item_factors, r.start) for r in rows]
    item_acc = [(item_accum, r.start) for r in rows]
    terms = [()] * CHUNKS
    held = []

    def part(c, after):
        whole = held if c == CHUNKS - 1 else []
        sent, *accums = parting_step(items[c][0], item_acc[c][0], terms[c], whole, after)
        items[c], terms[c] = (moved(sent, 1, 0), 0), ()
        return accums

    for step in range(SUB * INNER):
        sub_epoch = step // INNER
        rotates = step > 0 and step % INNER == 0
        if rotates:
            for c in range(1, CHUNKS - 1):
                held += part(c, [term, held[-1]])
        if step > 0:
            user_half = users.astype(jnp.bfloat16)
            grad_user = shrink * users
        for c in range(CHUNKS):
            if rotates and c == 1:
                accums = [moved(accum, 1, 0) for accum in part(CHUNKS - 1, [term])]
                item_acc = [(accums[d // LAST], d % LAST * size) for d in range(CHUNKS)]
            after = []
            if c == CHUNKS - 1 and step % INNER == INNER - 1 and sub_epoch < SUB - 1:
                held = part(0, [])
                after = held[:]
            if step == 0:
                if c % FIRST:
                    terms[c] = terms[c - 1]
                    continue
                both = slice(rows[c].start, rows[c + FIRST - 1].stop)
                if c == 0:
                    term, grad_user, user_half = first_pass(ratings, both, users, item_factors)
                else:
                    piece = (items[c], item_acc[c], (), 0)
                    term, grad_user = chunk_pass(ratings, 0, both, user_half, grad_user, [piece])
            else:
                taken = [c]
                if step == SUB * INNER - 1:
                    if c % LAST:
                        continue
                    taken = range(c, c + LAST)
                at = [d % FIRST * size if step == 1 else 0 for d in taken]
                term, grad_user, *updated = chunk_pass(
                    ratings, sub_epoch, slice(rows[c].start, rows[taken[-1]].stop), user_half, grad_user,
                    [(items[d], item_acc[d], terms[d], row) for d, row in zip(taken, at)], after,
                )
                if updated:
                    items[c], item_acc[c] = ((array, 0) for array in updated)
            terms[c] = group_terms(term)
        users, user_acc = adagrad(users, user_acc, grad_user)
    filled = []
    for c in range(0, CHUNKS, LAST):
        filled = [last_item_step(rows[c], item_factors.shape[0], items[c][0], item_acc[c][0], terms[c], filled)]
    return (users, filled[0])


def solution(mesh):
    in_specs = (
        P(None, ("loop", "grp"), None),
        P(("loop", "grp"), None),
        P(("loop", "grp"), None),
        P("loop", None),
        P("loop", None),
    )
    out_specs = (P(("loop", "grp"), None), P("loop", None))
    return jax.shard_map(local, mesh=mesh, in_specs=in_specs, out_specs=out_specs, check_vma=False)
```

```python
import functools

import jax
import jax.numpy as jnp
from jax import lax
from jax.experimental import pallas as pl
from jax.experimental.pallas import tpu as pltpu
from jax.sharding import PartitionSpec as P

SUB = 2
INNER = 2
CHUNKS = 4
FIRST = 2
LAST = 2
TILE = 256


shrink = 0.05
learn_rate = 0.2
tiny_eps = 1e-06


def moved(shard, loop_by, grp_by):
    loops, groups = lax.axis_size("loop"), lax.axis_size("grp")
    pairs = [
        (w * groups + g, (w + loop_by) % loops * groups + (g + grp_by) % groups)
        for w in range(loops)
        for g in range(groups)
    ]
    return lax.ppermute(shard, ("loop", "grp"), pairs)


def adagrad(param, accum, grad):
    accum = accum + grad * grad
    return (param - learn_rate * grad * lax.rsqrt(accum + tiny_eps), accum)


def group_terms(term):
    if lax.axis_size("grp") == 2:
        return (term, moved(term, 0, 1))
    return (lax.psum(term, "grp"),)


def item_step(items, accum, terms):
    items = items.astype(jnp.float32)
    grad = sum(term.astype(jnp.float32) for term in terms) + shrink * items
    return adagrad(items, accum.astype(jnp.float32), grad)


def chunk_tile(half, half_t, items, rate):
    item_half = items.astype(jnp.bfloat16)
    predicted = lax.dot_general(
        half, item_half, (((1,), (1,)), ((), ())), preferred_element_type=jnp.float32
    )
    rate = rate.astype(jnp.float32)
    resid = jnp.where(jnp.abs(rate) > 0.25, rate - predicted, 0.0).astype(jnp.bfloat16)
    term = jnp.dot(half_t, resid, preferred_element_type=jnp.float32)
    return (-term).T.astype(jnp.bfloat16), jnp.dot(resid, item_half, preferred_element_type=jnp.float32)


def params(mib=16):
    return pltpu.CompilerParams(vmem_limit_bytes=mib * 2**20)


def cost(users, items, rank):
    return pl.CostEstimate(
        flops=6 * users * items * rank, bytes_accessed=2 * users * items, transcendentals=0
    )


WHOLE = pl.BlockSpec(memory_space=pltpu.VMEM)
AWAY = pl.BlockSpec(memory_space=pltpu.HBM)


def first_kernel(column, rate_hbm, items_hbm, users_hbm, term_out, grad_out, half_out, *scratch):
    users_ref, rate_ref, items_ref, sems = scratch
    load_users = pltpu.make_async_copy(users_hbm, users_ref, sems.at[2, 0])
    load_users.start()
    tiles = range(term_out.shape[0] // TILE)
    loads = []
    for t in tiles:
        at = pl.ds(column + t * TILE, TILE)
        loads.append(
            (
                pltpu.make_async_copy(items_hbm.at[at, :], items_ref.at[t], sems.at[0, t]),
                pltpu.make_async_copy(rate_hbm.at[0, :, at], rate_ref.at[t], sems.at[1, t]),
            )
        )
        for load in loads[-1]:
            load.start()
    load_users.wait()
    grad = shrink * users_ref[...]
    half = users_ref[...].astype(jnp.bfloat16)
    half_t = half.T
    half_out[...] = half
    for t in tiles:
        for load in loads[t]:
            load.wait()
        term, part = chunk_tile(half, half_t, items_ref[t], rate_ref[t])
        term_out[pl.ds(t * TILE, TILE), :] = term
        grad = grad - part
    grad_out[...] = grad


def first_pass(ratings, rows, users, items):
    size, (n_users, rank) = rows.stop - rows.start, users.shape
    return pl.pallas_call(
        functools.partial(first_kernel, rows.start),
        out_shape=[
            jax.ShapeDtypeStruct((size, rank), jnp.bfloat16),
            jax.ShapeDtypeStruct(users.shape, jnp.float32),
            jax.ShapeDtypeStruct(users.shape, jnp.bfloat16),
        ],
        in_specs=[AWAY] * 3,
        out_specs=[WHOLE] * 3,
        scratch_shapes=[
            pltpu.VMEM(users.shape, jnp.float32),
            pltpu.VMEM((size // TILE, n_users, TILE), jnp.bfloat16),
            pltpu.VMEM((size // TILE, TILE, rank), jnp.float32),
            pltpu.SemaphoreType.DMA((3, size // TILE)),
        ],
        compiler_params=params(62),
        cost_estimate=cost(n_users, size, rank),
    )(ratings, items, users)


def chunk_kernel(sub_epoch, column, size, places, rate_ref, half_ref, grad_ref, *refs):
    half = half_ref[...]
    half_t = half.T
    grad = grad_ref[...]
    term_out, grad_out, *updated = refs[-4:] if places[0][0] else refs[-2:]
    for piece, (n_terms, items_at, accum_at, terms_at) in enumerate(places):
        items_ref, *refs = refs
        if n_terms:
            accum_ref, *refs = refs
            term_refs, refs = refs[:n_terms], refs[n_terms:]
        for start in range(0, size, TILE):
            at = pl.ds(piece * size + start, TILE)
            items = items_ref[pl.ds(items_at + start, TILE), :]
            if n_terms:
                accum = accum_ref[pl.ds(accum_at + start, TILE), :]
                terms = [ref[pl.ds(terms_at + start, TILE), :] for ref in term_refs]
                items, accum = item_step(items, accum, terms)
                updated[0][at, :] = items
                updated[1][at, :] = accum
            rate = rate_ref[sub_epoch, :, pl.ds(column + piece * size + start, TILE)]
            term_out[at, :], part = chunk_tile(half, half_t, items, rate)
            grad = grad - part
    grad_out[...] = grad


def chunk_pass(ratings, sub_epoch, rows, half, grad, pieces, after=()):
    total, rank = rows.stop - rows.start, half.shape[1]
    out_shape = [
        jax.ShapeDtypeStruct((total, rank), jnp.bfloat16),
        jax.ShapeDtypeStruct(grad.shape, jnp.float32),
    ]
    operands, places = [ratings, half, grad], []
    for items, accum, terms, terms_at in pieces:
        operands += [items[0], accum[0], *terms] if terms else [items[0]]
        places.append((len(terms), items[1], accum[1], terms_at))
    if places[0][0]:
        out_shape += [jax.ShapeDtypeStruct((total, rank), jnp.float32)] * 2
    return pl.pallas_call(
        functools.partial(chunk_kernel, sub_epoch, rows.start, total // len(pieces), places),
        out_shape=out_shape,
        in_specs=[WHOLE] * len(operands) + [pl.BlockSpec(memory_space=pl.ANY)] * len(after),
        out_specs=[WHOLE] * len(out_shape),
        compiler_params=params(),
        cost_estimate=cost(half.shape[0], total, rank),
    )(*operands, *after)


def parting_kernel(n_terms, n_behind, items_ref, accum_ref, *refs):
    size = items_ref.shape[0]
    items, accum = item_step(items_ref[...], accum_ref[...], [ref[...] for ref in refs[:n_terms]])
    sent, accum_out = refs[-2:]
    sent[pl.ds(0, size), :] = items.astype(jnp.bfloat16)
    if n_behind:
        sent[pl.ds(size, size), :] = refs[n_terms][...]
    accum_out[...] = accum.astype(jnp.bfloat16)


def parting_step(items, accum, terms, behind, after):
    size, rank = items.shape
    return pl.pallas_call(
        functools.partial(parting_kernel, len(terms), len(behind)),
        out_shape=[
            jax.ShapeDtypeStruct((size * (1 + len(behind)), rank), jnp.bfloat16),
            jax.ShapeDtypeStruct((size, rank), jnp.bfloat16),
        ],
        in_specs=[WHOLE] * (2 + len(terms) + len(behind)) + [pl.BlockSpec(memory_space=pl.ANY)] * len(after),
        out_specs=[WHOLE] * 2,
        compiler_params=params(),
        cost_estimate=cost(1, size, rank),
    )(items, accum, *terms, *behind, *after)


def last_kernel(n_terms, row, items_ref, accum_ref, *refs):
    out_hbm, out_ref, sems = refs[-3:]
    stores = []
    for t in range(items_ref.shape[0] // TILE):
        at = pl.ds(t * TILE, TILE)
        out_ref[at, :], _ = item_step(items_ref[at, :], accum_ref[at, :], [ref[at, :] for ref in refs[:n_terms]])
        stores.append(
            pltpu.make_async_copy(out_ref.at[at, :], out_hbm.at[pl.ds(row + t * TILE, TILE), :], sems.at[t])
        )
        stores[-1].start()
    for store in stores:
        store.wait()


def last_item_step(rows, n_items, items, accum, terms, filled):
    size, rank = items.shape
    return pl.pallas_call(
        functools.partial(last_kernel, len(terms), rows.start),
        out_shape=jax.ShapeDtypeStruct((n_items, rank), jnp.float32),
        in_specs=[WHOLE] * (2 + len(terms)) + [AWAY] * len(filled),
        out_specs=AWAY,
        scratch_shapes=[
            pltpu.VMEM((size, rank), jnp.float32),
            pltpu.SemaphoreType.DMA((size // TILE,)),
        ],
        input_output_aliases={2 + len(terms): 0} if filled else {},
        compiler_params=params(),
        cost_estimate=cost(1, size, rank),
    )(items, accum, *terms, *filled)


def local(ratings, user_factors, user_accum, item_factors, item_accum):
    users = user_factors
    user_acc = user_accum
    size = item_factors.shape[0] // CHUNKS
    rows = [slice(c * size, (c + 1) * size) for c in range(CHUNKS)]
    items = [(item_factors, r.start) for r in rows]
    item_acc = [(item_accum, r.start) for r in rows]
    terms = [()] * CHUNKS
    behind = []

    def part(c, after):
        nonlocal behind
        sent, accum = parting_step(items[c][0], item_acc[c][0], terms[c], behind, after)
        items[c] = (moved(sent, 1, 0), 0)
        if c > 0:
            item_acc[c - 1] = (items[c][0], size)
        behind, terms[c] = [accum], ()
        return [sent]

    for step in range(SUB * INNER):
        sub_epoch = step // INNER
        rotates = step > 0 and step % INNER == 0
        if rotates:
            for c in range(1, CHUNKS - 1):
                part(c, [term])
        if step > 0:
            user_half = users.astype(jnp.bfloat16)
            grad_user = shrink * users
        for c in range(CHUNKS):
            if rotates and c == 1:
                part(CHUNKS - 1, [term])
                item_acc[CHUNKS - 1] = (moved(behind[0], 1, 0), 0)
            after = []
            if c == CHUNKS - 1 and step % INNER == INNER - 1 and sub_epoch < SUB - 1:
                behind = []
                after = part(0, [])
            elif c == FIRST - 1 and step == 1:
                after = [terms[FIRST][-1]]
            if step == 0:
                if c % FIRST:
                    terms[c] = terms[c - 1]
                    continue
                both = slice(rows[c].start, rows[c + FIRST - 1].stop)
                if c == 0:
                    term, grad_user, user_half = first_pass(ratings, both, users, item_factors)
                else:
                    piece = (items[c], item_acc[c], (), 0)
                    term, grad_user = chunk_pass(ratings, 0, both, user_half, grad_user, [piece])
            else:
                taken = [c]
                if step == SUB * INNER - 1:
                    if c % LAST:
                        continue
                    taken = range(c, c + LAST)
                at = [d % FIRST * size if step == 1 else 0 for d in taken]
                term, grad_user, *updated = chunk_pass(
                    ratings, sub_epoch, slice(rows[c].start, rows[taken[-1]].stop), user_half, grad_user,
                    [(items[d], item_acc[d], terms[d], row) for d, row in zip(taken, at)], after,
                )
                if updated:
                    items[c], item_acc[c] = ((array, 0) for array in updated)
            terms[c] = group_terms(term)
        users, user_acc = adagrad(users, user_acc, grad_user)
    filled = []
    for c in range(0, CHUNKS, LAST):
        filled = [last_item_step(rows[c], item_factors.shape[0], items[c][0], item_acc[c][0], terms[c], filled)]
    return (users, filled[0])


def solution(mesh):
    in_specs = (
        P(None, ("loop", "grp"), None),
        P(("loop", "grp"), None),
        P(("loop", "grp"), None),
        P("loop", None),
        P("loop", None),
    )
    out_specs = (P(("loop", "grp"), None), P("loop", None))
    return jax.shard_map(local, mesh=mesh, in_specs=in_specs, out_specs=out_specs, check_vma=False)
```

```python
import functools

import jax
import jax.numpy as jnp
from jax import lax
from jax.experimental import pallas as pl
from jax.experimental.pallas import tpu as pltpu
from jax.sharding import PartitionSpec as P

SUB = 2
INNER = 2
CHUNKS = 4
FIRST = 2
LAST = 2
TILE = 256


shrink = 0.05
learn_rate = 0.2
tiny_eps = 1e-06


def moved(shard, loop_by, grp_by):
    loops, groups = lax.axis_size("loop"), lax.axis_size("grp")
    pairs = [
        (w * groups + g, (w + loop_by) % loops * groups + (g + grp_by) % groups)
        for w in range(loops)
        for g in range(groups)
    ]
    return lax.ppermute(shard, ("loop", "grp"), pairs)


def adagrad(param, accum, grad):
    accum = accum + grad * grad
    return (param - learn_rate * grad * lax.rsqrt(accum + tiny_eps), accum)


def group_terms(term):
    if lax.axis_size("grp") == 2:
        return (term, moved(term, 0, 1))
    return (lax.psum(term, "grp"),)


def item_step(items, accum, terms):
    items = items.astype(jnp.float32)
    grad = sum(term.astype(jnp.float32) for term in terms) + shrink * items
    return adagrad(items, accum.astype(jnp.float32), grad)


def chunk_tile(half, half_t, items, rate):
    item_half = items.astype(jnp.bfloat16)
    predicted = lax.dot_general(
        half, item_half, (((1,), (1,)), ((), ())), preferred_element_type=jnp.float32
    )
    rate = rate.astype(jnp.float32)
    resid = jnp.where(jnp.abs(rate) > 0.25, rate - predicted, 0.0).astype(jnp.bfloat16)
    term = jnp.dot(half_t, resid, preferred_element_type=jnp.float32)
    return (-term).T.astype(jnp.bfloat16), jnp.dot(resid, item_half, preferred_element_type=jnp.float32)


def params(mib=16):
    return pltpu.CompilerParams(vmem_limit_bytes=mib * 2**20)


def cost(users, items, rank):
    return pl.CostEstimate(
        flops=6 * users * items * rank, bytes_accessed=2 * users * items, transcendentals=0
    )


WHOLE = pl.BlockSpec(memory_space=pltpu.VMEM)
AWAY = pl.BlockSpec(memory_space=pltpu.HBM)


def first_kernel(column, rate_hbm, items_hbm, users_hbm, term_out, grad_out, half_out, *scratch):
    users_ref, rate_ref, items_ref, sems = scratch
    load_users = pltpu.make_async_copy(users_hbm, users_ref, sems.at[2, 0])
    load_users.start()
    tiles = range(term_out.shape[0] // TILE)
    loads = []
    for t in tiles:
        at = pl.ds(column + t * TILE, TILE)
        loads.append(
            (
                pltpu.make_async_copy(items_hbm.at[at, :], items_ref.at[t], sems.at[0, t]),
                pltpu.make_async_copy(rate_hbm.at[0, :, at], rate_ref.at[t], sems.at[1, t]),
            )
        )
        for load in loads[-1]:
            load.start()
    load_users.wait()
    grad = shrink * users_ref[...]
    half = users_ref[...].astype(jnp.bfloat16)
    half_t = half.T
    half_out[...] = half
    for t in tiles:
        for load in loads[t]:
            load.wait()
        term, part = chunk_tile(half, half_t, items_ref[t], rate_ref[t])
        term_out[pl.ds(t * TILE, TILE), :] = term
        grad = grad - part
    grad_out[...] = grad


def first_pass(ratings, rows, users, items):
    size, (n_users, rank) = rows.stop - rows.start, users.shape
    return pl.pallas_call(
        functools.partial(first_kernel, rows.start),
        out_shape=[
            jax.ShapeDtypeStruct((size, rank), jnp.bfloat16),
            jax.ShapeDtypeStruct(users.shape, jnp.float32),
            jax.ShapeDtypeStruct(users.shape, jnp.bfloat16),
        ],
        in_specs=[AWAY] * 3,
        out_specs=[WHOLE] * 3,
        scratch_shapes=[
            pltpu.VMEM(users.shape, jnp.float32),
            pltpu.VMEM((size // TILE, n_users, TILE), jnp.bfloat16),
            pltpu.VMEM((size // TILE, TILE, rank), jnp.float32),
            pltpu.SemaphoreType.DMA((3, size // TILE)),
        ],
        compiler_params=params(62),
        cost_estimate=cost(n_users, size, rank),
    )(ratings, items, users)


def chunk_kernel(sub_epoch, column, size, places, rate_ref, half_ref, grad_ref, *refs):
    half = half_ref[...]
    half_t = half.T
    grad = grad_ref[...]
    term_out, grad_out, *updated = refs[-4:] if places[0][0] else refs[-2:]
    for piece, (n_terms, items_at, accum_at, terms_at) in enumerate(places):
        items_ref, *refs = refs
        if n_terms:
            accum_ref, *refs = refs
            term_refs, refs = refs[:n_terms], refs[n_terms:]
        for start in range(0, size, TILE):
            at = pl.ds(piece * size + start, TILE)
            items = items_ref[pl.ds(items_at + start, TILE), :]
            if n_terms:
                accum = accum_ref[pl.ds(accum_at + start, TILE), :]
                terms = [ref[pl.ds(terms_at + start, TILE), :] for ref in term_refs]
                items, accum = item_step(items, accum, terms)
                updated[0][at, :] = items
                updated[1][at, :] = accum
            rate = rate_ref[sub_epoch, :, pl.ds(column + piece * size + start, TILE)]
            term_out[at, :], part = chunk_tile(half, half_t, items, rate)
            grad = grad - part
    grad_out[...] = grad


def chunk_pass(ratings, sub_epoch, rows, half, grad, pieces, after=()):
    total, rank = rows.stop - rows.start, half.shape[1]
    out_shape = [
        jax.ShapeDtypeStruct((total, rank), jnp.bfloat16),
        jax.ShapeDtypeStruct(grad.shape, jnp.float32),
    ]
    operands, places = [ratings, half, grad], []
    for items, accum, terms, terms_at in pieces:
        operands += [items[0], accum[0], *terms] if terms else [items[0]]
        places.append((len(terms), items[1], accum[1], terms_at))
    if places[0][0]:
        out_shape += [jax.ShapeDtypeStruct((total, rank), jnp.float32)] * 2
    return pl.pallas_call(
        functools.partial(chunk_kernel, sub_epoch, rows.start, total // len(pieces), places),
        out_shape=out_shape,
        in_specs=[WHOLE] * len(operands) + [pl.BlockSpec(memory_space=pl.ANY)] * len(after),
        out_specs=[WHOLE] * len(out_shape),
        compiler_params=params(),
        cost_estimate=cost(half.shape[0], total, rank),
    )(*operands, *after)


def parting_kernel(n_terms, n_behind, items_ref, accum_ref, *refs):
    size = items_ref.shape[0]
    items, accum = item_step(items_ref[...], accum_ref[...], [ref[...] for ref in refs[:n_terms]])
    sent, accum_out = refs[-2:]
    sent[pl.ds(0, size), :] = items.astype(jnp.bfloat16)
    if n_behind:
        sent[pl.ds(size, size), :] = refs[n_terms][...]
    accum_out[...] = accum.astype(jnp.bfloat16)


def parting_step(items, accum, terms, behind, after):
    size, rank = items.shape
    return pl.pallas_call(
        functools.partial(parting_kernel, len(terms), len(behind)),
        out_shape=[
            jax.ShapeDtypeStruct((size * (1 + len(behind)), rank), jnp.bfloat16),
            jax.ShapeDtypeStruct((size, rank), jnp.bfloat16),
        ],
        in_specs=[WHOLE] * (2 + len(terms) + len(behind)) + [pl.BlockSpec(memory_space=pl.ANY)] * len(after),
        out_specs=[WHOLE] * 2,
        compiler_params=params(),
        cost_estimate=cost(1, size, rank),
    )(items, accum, *terms, *behind, *after)


def last_kernel(n_terms, row, items_ref, accum_ref, *refs):
    out_hbm, out_ref, sems = refs[-3:]
    stores = []
    for t in range(items_ref.shape[0] // TILE):
        at = pl.ds(t * TILE, TILE)
        out_ref[at, :], _ = item_step(items_ref[at, :], accum_ref[at, :], [ref[at, :] for ref in refs[:n_terms]])
        stores.append(
            pltpu.make_async_copy(out_ref.at[at, :], out_hbm.at[pl.ds(row + t * TILE, TILE), :], sems.at[t])
        )
        stores[-1].start()
    for store in stores:
        store.wait()


def last_item_step(rows, n_items, items, accum, terms, filled):
    size, rank = items.shape
    return pl.pallas_call(
        functools.partial(last_kernel, len(terms), rows.start),
        out_shape=jax.ShapeDtypeStruct((n_items, rank), jnp.float32),
        in_specs=[WHOLE] * (2 + len(terms)) + [AWAY] * len(filled),
        out_specs=AWAY,
        scratch_shapes=[
            pltpu.VMEM((size, rank), jnp.float32),
            pltpu.SemaphoreType.DMA((size // TILE,)),
        ],
        input_output_aliases={2 + len(terms): 0} if filled else {},
        compiler_params=params(),
        cost_estimate=cost(1, size, rank),
    )(items, accum, *terms, *filled)


def local(ratings, user_factors, user_accum, item_factors, item_accum):
    users = user_factors
    user_acc = user_accum
    size = item_factors.shape[0] // CHUNKS
    rows = [slice(c * size, (c + 1) * size) for c in range(CHUNKS)]
    items = [(item_factors, r.start) for r in rows]
    item_acc = [(item_accum, r.start) for r in rows]
    terms = [()] * CHUNKS
    behind = []

    def part(c, after):
        nonlocal behind
        sent, accum = parting_step(items[c][0], item_acc[c][0], terms[c], behind, after)
        items[c] = (moved(sent, 1, 0), 0)
        if c > 0:
            item_acc[c - 1] = (items[c][0], size)
        behind, terms[c] = [accum], ()
        return [sent]

    for step in range(SUB * INNER):
        sub_epoch = step // INNER
        rotates = step > 0 and step % INNER == 0
        if rotates:
            for c in range(1, CHUNKS - 1):
                part(c, [term])
        if step > 0:
            user_half = users.astype(jnp.bfloat16)
            grad_user = shrink * users
        for c in range(CHUNKS):
            if rotates and c == 1:
                part(CHUNKS - 1, [term])
                item_acc[CHUNKS - 1] = (moved(behind[0], 1, 0), 0)
            after = []
            if c == CHUNKS - 2 and step % INNER == INNER - 1 and sub_epoch < SUB - 1:
                behind = []
                after = part(0, [])
            elif c == FIRST - 1 and step == 1:
                after = [terms[FIRST][-1]]
            if step == 0:
                if c % FIRST:
                    terms[c] = terms[c - 1]
                    continue
                both = slice(rows[c].start, rows[c + FIRST - 1].stop)
                if c == 0:
                    term, grad_user, user_half = first_pass(ratings, both, users, item_factors)
                else:
                    piece = (items[c], item_acc[c], (), 0)
                    term, grad_user = chunk_pass(ratings, 0, both, user_half, grad_user, [piece])
            else:
                taken = [c]
                if step == SUB * INNER - 1:
                    if c % LAST:
                        continue
                    taken = range(c, c + LAST)
                at = [d % FIRST * size if step == 1 else 0 for d in taken]
                term, grad_user, *updated = chunk_pass(
                    ratings, sub_epoch, slice(rows[c].start, rows[taken[-1]].stop), user_half, grad_user,
                    [(items[d], item_acc[d], terms[d], row) for d, row in zip(taken, at)], after,
                )
                if updated:
                    items[c], item_acc[c] = ((array, 0) for array in updated)
            terms[c] = group_terms(term)
        users, user_acc = adagrad(users, user_acc, grad_user)
    filled = []
    for c in range(0, CHUNKS, LAST):
        filled = [last_item_step(rows[c], item_factors.shape[0], items[c][0], item_acc[c][0], terms[c], filled)]
    return (users, filled[0])


def solution(mesh):
    in_specs = (
        P(None, ("loop", "grp"), None),
        P(("loop", "grp"), None),
        P(("loop", "grp"), None),
        P("loop", None),
        P("loop", None),
    )
    out_specs = (P(("loop", "grp"), None), P("loop", None))
    return jax.shard_map(local, mesh=mesh, in_specs=in_specs, out_specs=out_specs, check_vma=False)
```

```python
import functools

import jax
import jax.numpy as jnp
from jax import lax
from jax.experimental import pallas as pl
from jax.experimental.pallas import tpu as pltpu
from jax.sharding import PartitionSpec as P

SUB = 2
INNER = 2
CHUNKS = 4
FIRST = 2
LAST = 2
TILE = 256


shrink = 0.05
learn_rate = 0.2
tiny_eps = 1e-06


def moved(shard, loop_by, grp_by):
    loops, groups = lax.axis_size("loop"), lax.axis_size("grp")
    pairs = [
        (w * groups + g, (w + loop_by) % loops * groups + (g + grp_by) % groups)
        for w in range(loops)
        for g in range(groups)
    ]
    return lax.ppermute(shard, ("loop", "grp"), pairs)


def adagrad(param, accum, grad):
    accum = accum + grad * grad
    return (param - learn_rate * grad * lax.rsqrt(accum + tiny_eps), accum)


def group_terms(term):
    if lax.axis_size("grp") == 2:
        return (term, moved(term, 0, 1))
    return (lax.psum(term, "grp"),)


def item_step(items, accum, terms):
    items = items.astype(jnp.float32)
    grad = sum(term.astype(jnp.float32) for term in terms) + shrink * items
    return adagrad(items, accum.astype(jnp.float32), grad)


def chunk_tile(half, half_t, items, rate):
    item_half = items.astype(jnp.bfloat16)
    predicted = lax.dot_general(
        half, item_half, (((1,), (1,)), ((), ())), preferred_element_type=jnp.float32
    )
    rate = rate.astype(jnp.float32)
    resid = jnp.where(jnp.abs(rate) > 0.25, rate - predicted, 0.0).astype(jnp.bfloat16)
    term = jnp.dot(half_t, resid, preferred_element_type=jnp.float32)
    return (-term).T.astype(jnp.bfloat16), jnp.dot(resid, item_half, preferred_element_type=jnp.float32)


def params(mib=16):
    return pltpu.CompilerParams(vmem_limit_bytes=mib * 2**20)


def cost(users, items, rank):
    return pl.CostEstimate(
        flops=6 * users * items * rank, bytes_accessed=2 * users * items, transcendentals=0
    )


WHOLE = pl.BlockSpec(memory_space=pltpu.VMEM)
AWAY = pl.BlockSpec(memory_space=pltpu.HBM)


def first_kernel(column, rate_hbm, items_hbm, users_hbm, term_out, grad_out, *scratch):
    users_ref, rate_ref, items_ref, sems = scratch
    load_users = pltpu.make_async_copy(users_hbm, users_ref, sems.at[2, 0])
    load_users.start()
    tiles = range(term_out.shape[0] // TILE)
    loads = []
    for t in tiles:
        at = pl.ds(column + t * TILE, TILE)
        loads.append(
            (
                pltpu.make_async_copy(items_hbm.at[at, :], items_ref.at[t], sems.at[0, t]),
                pltpu.make_async_copy(rate_hbm.at[0, :, at], rate_ref.at[t], sems.at[1, t]),
            )
        )
        for load in loads[-1]:
            load.start()
    load_users.wait()
    grad = shrink * users_ref[...]
    half = users_ref[...].astype(jnp.bfloat16)
    half_t = half.T
    for t in tiles:
        for load in loads[t]:
            load.wait()
        term, part = chunk_tile(half, half_t, items_ref[t], rate_ref[t])
        term_out[pl.ds(t * TILE, TILE), :] = term
        grad = grad - part
    grad_out[...] = grad


def first_pass(ratings, rows, users, items):
    size, (n_users, rank) = rows.stop - rows.start, users.shape
    return pl.pallas_call(
        functools.partial(first_kernel, rows.start),
        out_shape=[
            jax.ShapeDtypeStruct((size, rank), jnp.bfloat16),
            jax.ShapeDtypeStruct(users.shape, jnp.float32),
        ],
        in_specs=[AWAY] * 3,
        out_specs=[WHOLE] * 2,
        scratch_shapes=[
            pltpu.VMEM(users.shape, jnp.float32),
            pltpu.VMEM((size // TILE, n_users, TILE), jnp.bfloat16),
            pltpu.VMEM((size // TILE, TILE, rank), jnp.float32),
            pltpu.SemaphoreType.DMA((3, size // TILE)),
        ],
        compiler_params=params(62),
        cost_estimate=cost(n_users, size, rank),
    )(ratings, items, users)


def chunk_kernel(sub_epoch, column, size, places, rate_ref, half_ref, grad_ref, *refs):
    half = half_ref[...].astype(jnp.bfloat16)
    half_t = half.T
    grad = grad_ref[...]
    term_out, grad_out, *updated = refs[-4:] if places[0][0] else refs[-2:]
    for piece, (n_terms, items_at, accum_at, terms_at) in enumerate(places):
        items_ref, *refs = refs
        if n_terms:
            accum_ref, *refs = refs
            term_refs, refs = refs[:n_terms], refs[n_terms:]
        for start in range(0, size, TILE):
            at = pl.ds(piece * size + start, TILE)
            items = items_ref[pl.ds(items_at + start, TILE), :]
            if n_terms:
                accum = accum_ref[pl.ds(accum_at + start, TILE), :]
                terms = [ref[pl.ds(terms_at + start, TILE), :] for ref in term_refs]
                items, accum = item_step(items, accum, terms)
                updated[0][at, :] = items
                updated[1][at, :] = accum
            rate = rate_ref[sub_epoch, :, pl.ds(column + piece * size + start, TILE)]
            term_out[at, :], part = chunk_tile(half, half_t, items, rate)
            grad = grad - part
    grad_out[...] = grad


def chunk_pass(ratings, sub_epoch, rows, half, grad, pieces, after=()):
    total, rank = rows.stop - rows.start, half.shape[1]
    out_shape = [
        jax.ShapeDtypeStruct((total, rank), jnp.bfloat16),
        jax.ShapeDtypeStruct(grad.shape, jnp.float32),
    ]
    operands, places = [ratings, half, grad], []
    for items, accum, terms, terms_at in pieces:
        operands += [items[0], accum[0], *terms] if terms else [items[0]]
        places.append((len(terms), items[1], accum[1], terms_at))
    if places[0][0]:
        out_shape += [jax.ShapeDtypeStruct((total, rank), jnp.float32)] * 2
    return pl.pallas_call(
        functools.partial(chunk_kernel, sub_epoch, rows.start, total // len(pieces), places),
        out_shape=out_shape,
        in_specs=[WHOLE] * len(operands) + [pl.BlockSpec(memory_space=pl.ANY)] * len(after),
        out_specs=[WHOLE] * len(out_shape),
        compiler_params=params(),
        cost_estimate=cost(half.shape[0], total, rank),
    )(*operands, *after)


def parting_kernel(n_terms, n_behind, items_ref, accum_ref, *refs):
    size = items_ref.shape[0]
    items, accum = item_step(items_ref[...], accum_ref[...], [ref[...] for ref in refs[:n_terms]])
    sent, accum_out = refs[-2:]
    sent[pl.ds(0, size), :] = items.astype(jnp.bfloat16)
    if n_behind:
        sent[pl.ds(size, size), :] = refs[n_terms][...]
    accum_out[...] = accum.astype(jnp.bfloat16)


def parting_step(items, accum, terms, behind, after):
    size, rank = items.shape
    return pl.pallas_call(
        functools.partial(parting_kernel, len(terms), len(behind)),
        out_shape=[
            jax.ShapeDtypeStruct((size * (1 + len(behind)), rank), jnp.bfloat16),
            jax.ShapeDtypeStruct((size, rank), jnp.bfloat16),
        ],
        in_specs=[WHOLE] * (2 + len(terms) + len(behind)) + [pl.BlockSpec(memory_space=pl.ANY)] * len(after),
        out_specs=[WHOLE] * 2,
        compiler_params=params(),
        cost_estimate=cost(1, size, rank),
    )(items, accum, *terms, *behind, *after)


def last_kernel(n_terms, row, items_ref, accum_ref, *refs):
    out_hbm, out_ref, sems = refs[-3:]
    stores = []
    for t in range(items_ref.shape[0] // TILE):
        at = pl.ds(t * TILE, TILE)
        out_ref[at, :], _ = item_step(items_ref[at, :], accum_ref[at, :], [ref[at, :] for ref in refs[:n_terms]])
        stores.append(
            pltpu.make_async_copy(out_ref.at[at, :], out_hbm.at[pl.ds(row + t * TILE, TILE), :], sems.at[t])
        )
        stores[-1].start()
    for store in stores:
        store.wait()


def last_item_step(rows, n_items, items, accum, terms, filled):
    size, rank = items.shape
    return pl.pallas_call(
        functools.partial(last_kernel, len(terms), rows.start),
        out_shape=jax.ShapeDtypeStruct((n_items, rank), jnp.float32),
        in_specs=[WHOLE] * (2 + len(terms)) + [AWAY] * len(filled),
        out_specs=AWAY,
        scratch_shapes=[
            pltpu.VMEM((size, rank), jnp.float32),
            pltpu.SemaphoreType.DMA((size // TILE,)),
        ],
        input_output_aliases={2 + len(terms): 0} if filled else {},
        compiler_params=params(),
        cost_estimate=cost(1, size, rank),
    )(items, accum, *terms, *filled)


def local(ratings, user_factors, user_accum, item_factors, item_accum):
    users = user_factors
    user_acc = user_accum
    size = item_factors.shape[0] // CHUNKS
    rows = [slice(c * size, (c + 1) * size) for c in range(CHUNKS)]
    items = [(item_factors, r.start) for r in rows]
    item_acc = [(item_accum, r.start) for r in rows]
    terms = [()] * CHUNKS
    behind = []

    def part(c, after):
        nonlocal behind
        sent, accum = parting_step(items[c][0], item_acc[c][0], terms[c], behind, after)
        items[c] = (moved(sent, 1, 0), 0)
        if c > 0:
            item_acc[c - 1] = (items[c][0], size)
        behind, terms[c] = [accum], ()
        return [sent]

    for step in range(SUB * INNER):
        sub_epoch = step // INNER
        rotates = step > 0 and step % INNER == 0
        if rotates:
            for c in range(1, CHUNKS - 1):
                part(c, [term])
        if step > 0:
            user_half = users.astype(jnp.bfloat16)
            grad_user = shrink * users
        for c in range(CHUNKS):
            if rotates and c == 1:
                part(CHUNKS - 1, [term])
                item_acc[CHUNKS - 1] = (moved(behind[0], 1, 0), 0)
            after = []
            if c == CHUNKS - 1 and step % INNER == INNER - 1 and sub_epoch < SUB - 1:
                behind = []
                after = part(0, [])
            if step == 0:
                if c % FIRST:
                    terms[c] = terms[c - 1]
                    continue
                both = slice(rows[c].start, rows[c + FIRST - 1].stop)
                if c == 0:
                    term, grad_user = first_pass(ratings, both, users, item_factors)
                else:
                    piece = (items[c], item_acc[c], (), 0)
                    term, grad_user = chunk_pass(ratings, 0, both, users, grad_user, [piece])
            else:
                taken = [c]
                if step == SUB * INNER - 1:
                    if c % LAST:
                        continue
                    taken = range(c, c + LAST)
                at = [d % FIRST * size if step == 1 else 0 for d in taken]
                term, grad_user, *updated = chunk_pass(
                    ratings, sub_epoch, slice(rows[c].start, rows[taken[-1]].stop), user_half, grad_user,
                    [(items[d], item_acc[d], terms[d], row) for d, row in zip(taken, at)], after,
                )
                if updated:
                    items[c], item_acc[c] = ((array, 0) for array in updated)
            terms[c] = group_terms(term)
        users, user_acc = adagrad(users, user_acc, grad_user)
    filled = []
    for c in range(0, CHUNKS, LAST):
        filled = [last_item_step(rows[c], item_factors.shape[0], items[c][0], item_acc[c][0], terms[c], filled)]
    return (users, filled[0])


def solution(mesh):
    in_specs = (
        P(None, ("loop", "grp"), None),
        P(("loop", "grp"), None),
        P(("loop", "grp"), None),
        P("loop", None),
        P("loop", None),
    )
    out_specs = (P(("loop", "grp"), None), P("loop", None))
    return jax.shard_map(local, mesh=mesh, in_specs=in_specs, out_specs=out_specs, check_vma=False)
```

```python
import functools

import jax
import jax.numpy as jnp
from jax import lax
from jax.experimental import pallas as pl
from jax.experimental.pallas import tpu as pltpu
from jax.sharding import PartitionSpec as P

SUB = 2
INNER = 2
CHUNKS = 4
FIRST = 2
LAST = 2
TILE = 256


shrink = 0.05
learn_rate = 0.2
tiny_eps = 1e-06


def moved(shard, loop_by, grp_by):
    loops, groups = lax.axis_size("loop"), lax.axis_size("grp")
    pairs = [
        (w * groups + g, (w + loop_by) % loops * groups + (g + grp_by) % groups)
        for w in range(loops)
        for g in range(groups)
    ]
    return lax.ppermute(shard, ("loop", "grp"), pairs)


def adagrad(param, accum, grad):
    accum = accum + grad * grad
    return (param - learn_rate * grad * lax.rsqrt(accum + tiny_eps), accum)


def group_terms(term):
    if lax.axis_size("grp") == 2:
        return (term, moved(term, 0, 1))
    return (lax.psum(term, "grp"),)


def item_step(items, accum, terms):
    items = items.astype(jnp.float32)
    grad = sum(term.astype(jnp.float32) for term in terms) + shrink * items
    return adagrad(items, accum.astype(jnp.float32), grad)


def chunk_tile(half, half_t, items, rate):
    item_half = items.astype(jnp.bfloat16)
    predicted = lax.dot_general(
        half, item_half, (((1,), (1,)), ((), ())), preferred_element_type=jnp.float32
    )
    rate = rate.astype(jnp.float32)
    resid = jnp.where(jnp.abs(rate) > 0.25, rate - predicted, 0.0).astype(jnp.bfloat16)
    term = jnp.dot(half_t, resid, preferred_element_type=jnp.float32)
    return (-term).T.astype(jnp.bfloat16), jnp.dot(resid, item_half, preferred_element_type=jnp.float32)


def params(mib=16):
    return pltpu.CompilerParams(vmem_limit_bytes=mib * 2**20)


def cost(users, items, rank):
    return pl.CostEstimate(
        flops=6 * users * items * rank, bytes_accessed=2 * users * items, transcendentals=0
    )


WHOLE = pl.BlockSpec(memory_space=pltpu.VMEM)
AWAY = pl.BlockSpec(memory_space=pltpu.HBM)


def first_kernel(column, rate_hbm, items_hbm, users_hbm, term_out, grad_out, done_out, *scratch):
    users_ref, rate_ref, items_ref, sems = scratch
    done_out[...] = jnp.zeros(done_out.shape, done_out.dtype)
    load_users = pltpu.make_async_copy(users_hbm, users_ref, sems.at[2, 0])
    load_users.start()
    tiles = range(term_out.shape[0] // TILE)
    loads = []
    for t in tiles:
        at = pl.ds(column + t * TILE, TILE)
        loads.append(
            (
                pltpu.make_async_copy(items_hbm.at[at, :], items_ref.at[t], sems.at[0, t]),
                pltpu.make_async_copy(rate_hbm.at[0, :, at], rate_ref.at[t], sems.at[1, t]),
            )
        )
        for load in loads[-1]:
            load.start()
    load_users.wait()
    grad = shrink * users_ref[...]
    half = users_ref[...].astype(jnp.bfloat16)
    half_t = half.T
    for t in tiles:
        for load in loads[t]:
            load.wait()
        term, part = chunk_tile(half, half_t, items_ref[t], rate_ref[t])
        term_out[pl.ds(t * TILE, TILE), :] = term
        grad = grad - part
    grad_out[...] = grad


def first_pass(ratings, rows, users, items):
    size, (n_users, rank) = rows.stop - rows.start, users.shape
    return pl.pallas_call(
        functools.partial(first_kernel, rows.start),
        out_shape=[
            jax.ShapeDtypeStruct((size, rank), jnp.bfloat16),
            jax.ShapeDtypeStruct(users.shape, jnp.float32),
            jax.ShapeDtypeStruct((8, 128), jnp.float32),
        ],
        in_specs=[AWAY] * 3,
        out_specs=[WHOLE] * 3,
        scratch_shapes=[
            pltpu.VMEM(users.shape, jnp.float32),
            pltpu.VMEM((size // TILE, n_users, TILE), jnp.bfloat16),
            pltpu.VMEM((size // TILE, TILE, rank), jnp.float32),
            pltpu.SemaphoreType.DMA((3, size // TILE)),
        ],
        compiler_params=params(62),
        cost_estimate=cost(n_users, size, rank),
    )(ratings, items, users)


def chunk_kernel(sub_epoch, column, size, places, adds, rate_ref, half_ref, *refs):
    if adds:
        grad_ref, *refs = refs
    half = half_ref[...].astype(jnp.bfloat16)
    half_t = half.T
    grad = grad_ref[...] if adds else jnp.zeros(half.shape, jnp.float32)
    term_out, grad_out, *updated = refs[-4:] if places[0][0] else refs[-2:]
    for piece, (n_terms, items_at, accum_at, terms_at) in enumerate(places):
        items_ref, *refs = refs
        if n_terms:
            accum_ref, *refs = refs
            term_refs, refs = refs[:n_terms], refs[n_terms:]
        for start in range(0, size, TILE):
            at = pl.ds(piece * size + start, TILE)
            items = items_ref[pl.ds(items_at + start, TILE), :]
            if n_terms:
                accum = accum_ref[pl.ds(accum_at + start, TILE), :]
                terms = [ref[pl.ds(terms_at + start, TILE), :] for ref in term_refs]
                items, accum = item_step(items, accum, terms)
                updated[0][at, :] = items
                updated[1][at, :] = accum
            rate = rate_ref[sub_epoch, :, pl.ds(column + piece * size + start, TILE)]
            term_out[at, :], part = chunk_tile(half, half_t, items, rate)
            grad = grad - part
    grad_out[...] = grad


def chunk_pass(ratings, sub_epoch, rows, half, grad, pieces, after=()):
    total, rank = rows.stop - rows.start, half.shape[1]
    out_shape = [
        jax.ShapeDtypeStruct((total, rank), jnp.bfloat16),
        jax.ShapeDtypeStruct(half.shape, jnp.float32),
    ]
    operands, places = [ratings, half] + ([] if grad is None else [grad]), []
    for items, accum, terms, terms_at in pieces:
        operands += [items[0], accum[0], *terms] if terms else [items[0]]
        places.append((len(terms), items[1], accum[1], terms_at))
    if places[0][0]:
        out_shape += [jax.ShapeDtypeStruct((total, rank), jnp.float32)] * 2
    return pl.pallas_call(
        functools.partial(chunk_kernel, sub_epoch, rows.start, total // len(pieces), places, grad is not None),
        out_shape=out_shape,
        in_specs=[WHOLE] * len(operands) + [pl.BlockSpec(memory_space=pl.ANY)] * len(after),
        out_specs=[WHOLE] * len(out_shape),
        compiler_params=params(),
        cost_estimate=cost(half.shape[0], total, rank),
    )(*operands, *after)


def parting_kernel(n_terms, n_behind, items_ref, accum_ref, *refs):
    size = items_ref.shape[0]
    items, accum = item_step(items_ref[...], accum_ref[...], [ref[...] for ref in refs[:n_terms]])
    sent, accum_out = refs[-2:]
    sent[pl.ds(0, size), :] = items.astype(jnp.bfloat16)
    if n_behind:
        sent[pl.ds(size, size), :] = refs[n_terms][...]
    accum_out[...] = accum.astype(jnp.bfloat16)


def parting_step(items, accum, terms, behind, after):
    size, rank = items.shape
    return pl.pallas_call(
        functools.partial(parting_kernel, len(terms), len(behind)),
        out_shape=[
            jax.ShapeDtypeStruct((size * (1 + len(behind)), rank), jnp.bfloat16),
            jax.ShapeDtypeStruct((size, rank), jnp.bfloat16),
        ],
        in_specs=[WHOLE] * (2 + len(terms) + len(behind)) + [pl.BlockSpec(memory_space=pl.ANY)] * len(after),
        out_specs=[WHOLE] * 2,
        compiler_params=params(),
        cost_estimate=cost(1, size, rank),
    )(items, accum, *terms, *behind, *after)


def last_kernel(n_terms, row, items_ref, accum_ref, *refs):
    out_hbm, out_ref, sems = refs[-3:]
    stores = []
    for t in range(items_ref.shape[0] // TILE):
        at = pl.ds(t * TILE, TILE)
        out_ref[at, :], _ = item_step(items_ref[at, :], accum_ref[at, :], [ref[at, :] for ref in refs[:n_terms]])
        stores.append(
            pltpu.make_async_copy(out_ref.at[at, :], out_hbm.at[pl.ds(row + t * TILE, TILE), :], sems.at[t])
        )
        stores[-1].start()
    for store in stores:
        store.wait()


def last_item_step(rows, n_items, items, accum, terms, filled):
    size, rank = items.shape
    return pl.pallas_call(
        functools.partial(last_kernel, len(terms), rows.start),
        out_shape=jax.ShapeDtypeStruct((n_items, rank), jnp.float32),
        in_specs=[WHOLE] * (2 + len(terms)) + [AWAY] * len(filled),
        out_specs=AWAY,
        scratch_shapes=[
            pltpu.VMEM((size, rank), jnp.float32),
            pltpu.SemaphoreType.DMA((size // TILE,)),
        ],
        input_output_aliases={2 + len(terms): 0} if filled else {},
        compiler_params=params(),
        cost_estimate=cost(1, size, rank),
    )(items, accum, *terms, *filled)


def local(ratings, user_factors, user_accum, item_factors, item_accum):
    users = user_factors
    user_acc = user_accum
    size = item_factors.shape[0] // CHUNKS
    rows = [slice(c * size, (c + 1) * size) for c in range(CHUNKS)]
    items = [(item_factors, r.start) for r in rows]
    item_acc = [(item_accum, r.start) for r in rows]
    terms = [()] * CHUNKS
    behind = []

    def part(c, after):
        nonlocal behind
        sent, accum = parting_step(items[c][0], item_acc[c][0], terms[c], behind, after)
        items[c] = (moved(sent, 1, 0), 0)
        if c > 0:
            item_acc[c - 1] = (items[c][0], size)
        behind, terms[c] = [accum], ()
        return [sent]

    for step in range(SUB * INNER):
        sub_epoch = step // INNER
        rotates = step > 0 and step % INNER == 0
        if rotates:
            for c in range(1, CHUNKS - 1):
                part(c, [term])
        if step > 0:
            user_half = users.astype(jnp.bfloat16)
            grad_user = shrink * users
        for c in range(CHUNKS):
            if rotates and c == 1:
                part(CHUNKS - 1, [term])
                item_acc[CHUNKS - 1] = (moved(behind[0], 1, 0), 0)
            after = []
            if c == CHUNKS - 1 and step % INNER == INNER - 1 and sub_epoch < SUB - 1:
                behind = []
                after = part(0, [])
            if step == 0:
                if c % FIRST:
                    terms[c] = terms[c - 1]
                    continue
                both = slice(rows[c].start, rows[c + FIRST - 1].stop)
                if c == 0:
                    term, grad_user, done = first_pass(ratings, both, users, item_factors)
                else:
                    piece = (items[c], item_acc[c], (), 0)
                    term, more = chunk_pass(ratings, 0, both, users, None, [piece], [done])
                    grad_user = grad_user + more
            else:
                taken = [c]
                if step == SUB * INNER - 1:
                    if c % LAST:
                        continue
                    taken = range(c, c + LAST)
                at = [d % FIRST * size if step == 1 else 0 for d in taken]
                term, grad_user, *updated = chunk_pass(
                    ratings, sub_epoch, slice(rows[c].start, rows[taken[-1]].stop), user_half, grad_user,
                    [(items[d], item_acc[d], terms[d], row) for d, row in zip(taken, at)], after,
                )
                if updated:
                    items[c], item_acc[c] = ((array, 0) for array in updated)
            terms[c] = group_terms(term)
        users, user_acc = adagrad(users, user_acc, grad_user)
    filled = []
    for c in range(0, CHUNKS, LAST):
        filled = [last_item_step(rows[c], item_factors.shape[0], items[c][0], item_acc[c][0], terms[c], filled)]
    return (users, filled[0])


def solution(mesh):
    in_specs = (
        P(None, ("loop", "grp"), None),
        P(("loop", "grp"), None),
        P(("loop", "grp"), None),
        P("loop", None),
        P("loop", None),
    )
    out_specs = (P(("loop", "grp"), None), P("loop", None))
    return jax.shard_map(local, mesh=mesh, in_specs=in_specs, out_specs=out_specs, check_vma=False)
```

```python
import functools

import jax
import jax.numpy as jnp
from jax import lax
from jax.experimental import pallas as pl
from jax.experimental.pallas import tpu as pltpu
from jax.sharding import PartitionSpec as P

SUB = 2
INNER = 2
CHUNKS = 4
FIRST = 2
LAST = 2
TILE = 256


shrink = 0.05
learn_rate = 0.2
tiny_eps = 1e-06


def moved(shard, loop_by, grp_by):
    loops, groups = lax.axis_size("loop"), lax.axis_size("grp")
    pairs = [
        (w * groups + g, (w + loop_by) % loops * groups + (g + grp_by) % groups)
        for w in range(loops)
        for g in range(groups)
    ]
    return lax.ppermute(shard, ("loop", "grp"), pairs)


def adagrad(param, accum, grad):
    accum = accum + grad * grad
    return (param - learn_rate * grad * lax.rsqrt(accum + tiny_eps), accum)


def group_terms(term):
    if lax.axis_size("grp") == 2:
        return (term, moved(term, 0, 1))
    return (lax.psum(term, "grp"),)


def item_step(items, accum, terms):
    items = items.astype(jnp.float32)
    grad = sum(term.astype(jnp.float32) for term in terms) + shrink * items
    return adagrad(items, accum.astype(jnp.float32), grad)


def chunk_tile(half, half_t, items, rate):
    item_half = items.astype(jnp.bfloat16)
    predicted = lax.dot_general(
        half, item_half, (((1,), (1,)), ((), ())), preferred_element_type=jnp.float32
    )
    rate = rate.astype(jnp.float32)
    resid = jnp.where(jnp.abs(rate) > 0.25, rate - predicted, 0.0).astype(jnp.bfloat16)
    term = jnp.dot(half_t, resid, preferred_element_type=jnp.float32)
    return (-term).T.astype(jnp.bfloat16), jnp.dot(resid, item_half, preferred_element_type=jnp.float32)


def params(mib=16):
    return pltpu.CompilerParams(vmem_limit_bytes=mib * 2**20)


def cost(users, items, rank):
    return pl.CostEstimate(
        flops=6 * users * items * rank, bytes_accessed=2 * users * items, transcendentals=0
    )


WHOLE = pl.BlockSpec(memory_space=pltpu.VMEM)
AWAY = pl.BlockSpec(memory_space=pltpu.HBM)


def first_kernel(column, rate_hbm, items_hbm, users_hbm, term_out, grad_out, done_out, *scratch):
    users_ref, rate_ref, items_ref, sems = scratch
    done_out[...] = jnp.zeros(done_out.shape, done_out.dtype)
    load_users = pltpu.make_async_copy(users_hbm, users_ref, sems.at[2, 0])
    load_users.start()
    tiles = range(term_out.shape[0] // TILE)
    loads = []
    for t in tiles:
        at = pl.ds(column + t * TILE, TILE)
        loads.append(
            (
                pltpu.make_async_copy(items_hbm.at[at, :], items_ref.at[t], sems.at[0, t]),
                pltpu.make_async_copy(rate_hbm.at[0, :, at], rate_ref.at[t], sems.at[1, t]),
            )
        )
        for load in loads[-1]:
            load.start()
    load_users.wait()
    grad = shrink * users_ref[...]
    half = users_ref[...].astype(jnp.bfloat16)
    half_t = half.T
    for t in tiles:
        for load in loads[t]:
            load.wait()
        term, part = chunk_tile(half, half_t, items_ref[t], rate_ref[t])
        term_out[pl.ds(t * TILE, TILE), :] = term
        grad = grad - part
    grad_out[...] = grad


def first_pass(ratings, rows, users, items):
    size, (n_users, rank) = rows.stop - rows.start, users.shape
    return pl.pallas_call(
        functools.partial(first_kernel, rows.start),
        out_shape=[
            jax.ShapeDtypeStruct((size, rank), jnp.bfloat16),
            jax.ShapeDtypeStruct(users.shape, jnp.float32),
            jax.ShapeDtypeStruct((8, 128), jnp.float32),
        ],
        in_specs=[AWAY] * 3,
        out_specs=[WHOLE] * 3,
        scratch_shapes=[
            pltpu.VMEM(users.shape, jnp.float32),
            pltpu.VMEM((size // TILE, n_users, TILE), jnp.bfloat16),
            pltpu.VMEM((size // TILE, TILE, rank), jnp.float32),
            pltpu.SemaphoreType.DMA((3, size // TILE)),
        ],
        compiler_params=params(57),
        cost_estimate=cost(n_users, size, rank),
    )(ratings, items, users)


def chunk_kernel(sub_epoch, column, size, places, adds, rate_ref, half_ref, *refs):
    if adds:
        grad_ref, *refs = refs
    half = half_ref[...].astype(jnp.bfloat16)
    half_t = half.T
    grad = grad_ref[...] if adds else jnp.zeros(half.shape, jnp.float32)
    term_out, grad_out, *updated = refs[-4:] if places[0][0] else refs[-2:]
    for piece, (n_terms, items_at, accum_at, terms_at) in enumerate(places):
        items_ref, *refs = refs
        if n_terms:
            accum_ref, *refs = refs
            term_refs, refs = refs[:n_terms], refs[n_terms:]
        for start in range(0, size, TILE):
            at = pl.ds(piece * size + start, TILE)
            items = items_ref[pl.ds(items_at + start, TILE), :]
            if n_terms:
                accum = accum_ref[pl.ds(accum_at + start, TILE), :]
                terms = [ref[pl.ds(terms_at + start, TILE), :] for ref in term_refs]
                items, accum = item_step(items, accum, terms)
                updated[0][at, :] = items
                updated[1][at, :] = accum
            rate = rate_ref[sub_epoch, :, pl.ds(column + piece * size + start, TILE)]
            term_out[at, :], part = chunk_tile(half, half_t, items, rate)
            grad = grad - part
    grad_out[...] = grad


def chunk_pass(ratings, sub_epoch, rows, half, grad, pieces, after=()):
    total, rank = rows.stop - rows.start, half.shape[1]
    out_shape = [
        jax.ShapeDtypeStruct((total, rank), jnp.bfloat16),
        jax.ShapeDtypeStruct(half.shape, jnp.float32),
    ]
    operands, places = [ratings, half] + ([] if grad is None else [grad]), []
    for items, accum, terms, terms_at in pieces:
        operands += [items[0], accum[0], *terms] if terms else [items[0]]
        places.append((len(terms), items[1], accum[1], terms_at))
    if places[0][0]:
        out_shape += [jax.ShapeDtypeStruct((total, rank), jnp.float32)] * 2
    return pl.pallas_call(
        functools.partial(chunk_kernel, sub_epoch, rows.start, total // len(pieces), places, grad is not None),
        out_shape=out_shape,
        in_specs=[WHOLE] * len(operands) + [pl.BlockSpec(memory_space=pl.ANY)] * len(after),
        out_specs=[WHOLE] * len(out_shape),
        compiler_params=params(),
        cost_estimate=cost(half.shape[0], total, rank),
    )(*operands, *after)


def parting_kernel(n_terms, n_behind, items_ref, accum_ref, *refs):
    size = items_ref.shape[0]
    items, accum = item_step(items_ref[...], accum_ref[...], [ref[...] for ref in refs[:n_terms]])
    sent, accum_out = refs[-2:]
    sent[pl.ds(0, size), :] = items.astype(jnp.bfloat16)
    if n_behind:
        sent[pl.ds(size, size), :] = refs[n_terms][...]
    accum_out[...] = accum.astype(jnp.bfloat16)


def parting_step(items, accum, terms, behind, after):
    size, rank = items.shape
    return pl.pallas_call(
        functools.partial(parting_kernel, len(terms), len(behind)),
        out_shape=[
            jax.ShapeDtypeStruct((size * (1 + len(behind)), rank), jnp.bfloat16),
            jax.ShapeDtypeStruct((size, rank), jnp.bfloat16),
        ],
        in_specs=[WHOLE] * (2 + len(terms) + len(behind)) + [pl.BlockSpec(memory_space=pl.ANY)] * len(after),
        out_specs=[WHOLE] * 2,
        compiler_params=params(),
        cost_estimate=cost(1, size, rank),
    )(items, accum, *terms, *behind, *after)


def last_kernel(n_terms, row, items_ref, accum_ref, *refs):
    out_hbm, out_ref, sems = refs[-3:]
    stores = []
    for t in range(items_ref.shape[0] // TILE):
        at = pl.ds(t * TILE, TILE)
        out_ref[at, :], _ = item_step(items_ref[at, :], accum_ref[at, :], [ref[at, :] for ref in refs[:n_terms]])
        stores.append(
            pltpu.make_async_copy(out_ref.at[at, :], out_hbm.at[pl.ds(row + t * TILE, TILE), :], sems.at[t])
        )
        stores[-1].start()
    for store in stores:
        store.wait()


def last_item_step(rows, n_items, items, accum, terms, filled):
    size, rank = items.shape
    return pl.pallas_call(
        functools.partial(last_kernel, len(terms), rows.start),
        out_shape=jax.ShapeDtypeStruct((n_items, rank), jnp.float32),
        in_specs=[WHOLE] * (2 + len(terms)) + [AWAY] * len(filled),
        out_specs=AWAY,
        scratch_shapes=[
            pltpu.VMEM((size, rank), jnp.float32),
            pltpu.SemaphoreType.DMA((size // TILE,)),
        ],
        input_output_aliases={2 + len(terms): 0} if filled else {},
        compiler_params=params(),
        cost_estimate=cost(1, size, rank),
    )(items, accum, *terms, *filled)


def local(ratings, user_factors, user_accum, item_factors, item_accum):
    users = user_factors
    user_acc = user_accum
    size = item_factors.shape[0] // CHUNKS
    rows = [slice(c * size, (c + 1) * size) for c in range(CHUNKS)]
    items = [(item_factors, r.start) for r in rows]
    item_acc = [(item_accum, r.start) for r in rows]
    terms = [()] * CHUNKS
    behind = []

    def part(c, after):
        nonlocal behind
        sent, accum = parting_step(items[c][0], item_acc[c][0], terms[c], behind, after)
        items[c] = (moved(sent, 1, 0), 0)
        if c > 0:
            item_acc[c - 1] = (items[c][0], size)
        behind, terms[c] = [accum], ()
        return [sent]

    for step in range(SUB * INNER):
        sub_epoch = step // INNER
        rotates = step > 0 and step % INNER == 0
        if rotates:
            for c in range(1, CHUNKS - 1):
                part(c, [term])
        if step > 0:
            user_half = users.astype(jnp.bfloat16)
            grad_user = shrink * users
        for c in range(CHUNKS):
            if rotates and c == 1:
                part(CHUNKS - 1, [term])
                item_acc[CHUNKS - 1] = (moved(behind[0], 1, 0), 0)
            after = []
            if c == CHUNKS - 1 and step % INNER == INNER - 1 and sub_epoch < SUB - 1:
                behind = []
                after = part(0, [])
            if step == 0:
                if c % FIRST:
                    terms[c] = terms[c - 1]
                    continue
                both = slice(rows[c].start, rows[c + FIRST - 1].stop)
                if c == 0:
                    term, grad_user, done = first_pass(ratings, both, users, item_factors)
                else:
                    piece = (items[c], item_acc[c], (), 0)
                    term, more = chunk_pass(ratings, 0, both, users, None, [piece], [done])
                    grad_user = grad_user + more
            else:
                taken = [c]
                if step == SUB * INNER - 1:
                    if c % LAST:
                        continue
                    taken = range(c, c + LAST)
                at = [d % FIRST * size if step == 1 else 0 for d in taken]
                term, grad_user, *updated = chunk_pass(
                    ratings, sub_epoch, slice(rows[c].start, rows[taken[-1]].stop), user_half, grad_user,
                    [(items[d], item_acc[d], terms[d], row) for d, row in zip(taken, at)], after,
                )
                if updated:
                    items[c], item_acc[c] = ((array, 0) for array in updated)
            terms[c] = group_terms(term)
        users, user_acc = adagrad(users, user_acc, grad_user)
    filled = []
    for c in range(0, CHUNKS, LAST):
        filled = [last_item_step(rows[c], item_factors.shape[0], items[c][0], item_acc[c][0], terms[c], filled)]
    return (users, filled[0])


def solution(mesh):
    in_specs = (
        P(None, ("loop", "grp"), None),
        P(("loop", "grp"), None),
        P(("loop", "grp"), None),
        P("loop", None),
        P("loop", None),
    )
    out_specs = (P(("loop", "grp"), None), P("loop", None))
    return jax.shard_map(local, mesh=mesh, in_specs=in_specs, out_specs=out_specs, check_vma=False)
```
